128 devices in a mesh: row: 16 (over z, y), col: 8 (over x, core).
Axes of the slice: x: 4, y: 4, z: 4, core: 2. Of those that a mesh axis runs over, the one named last changes fastest.
Arguments:
- frames: bfloat16 [1048576, 1024], P(('row', 'col')), may hold values from -5 to 5
- frame_counts: int32 [128, 64], P(('row', 'col')), may hold values from 0 to 1000, as said below
- slot_ids: int32 [128, 64], P(('row', 'col')), may hold values from 0 to 4096, as said below
- seed_labels: int32 [4096], P(('row', 'col')), may hold values from 0 to 1023
- attn_query: bfloat16 [1024, 8], replicated, may hold values from -0.1875 to 0.1875
- emb_weight: bfloat16 [8192, 256], replicated, may hold values from -0.0625 to 0.0625
- plda_weight: bfloat16 [256, 256], replicated
Outputs:
- label_scores: float32 [4096, 256], P(('row', 'col'))
The draws below stay inside these ranges and needn't reach their ends.
Inputs may be any that keep to these rules, and one draw needn't show every extreme that they name: `slot_ids`: each utterance 0 to 4095 sits in exactly one slot whose frame count is positive; slots with count 0 hold 4096. Every utterance of owner o has its home block (utterance // 32) in o's grid column, that is with the same index along col as o; among one owner's utterances at most 4 have the same home block; each home block holds 32 utterances. `frame_counts`: an owner's live slots come first, their frames lie back to back from its first frame slot and sum to at most 8192; a live count is 100 or more. In each grid column, the owners of grid rows 4g to 4g + 3 hold 8, 24, 32 and 64 utterances in some order.
All inputs are finite; a program needn't handle non-finite values.
Results may differ from the reference program's by a relative error of at most 0.0034.
Values may be sent and summed in bfloat16 or wider, within the bound.
A program may use at most 64 MiB of HBM per device.

```python
import math
import jax
import jax.numpy as jnp
from jax import lax

D = 1024
HEADS = 8
E = 256
K = 256
U_HOME = 32
FPU = 256
LMIN = 100
LMAX = 1000
ITERS = 3
CAP = 4
U_CAP = 64
F_DEV = 8192
N = 4096
N_COL = 8


cluster_size = 16


def live_counts(key):
    owners = N // U_HOME
    groups = owners // (4 * N_COL)
    pattern = jnp.array([U_HOME // 4, 3 * U_HOME // 4, U_HOME, 2 * U_HOME], jnp.int32)
    scores = jax.random.randint(key, (groups, 4, N_COL), 0, 1 << 20) * 4 + jnp.arange(4, dtype=jnp.int32)[None, :, None]
    ranking = jnp.argsort(scores, axis=1)
    return pattern[ranking].reshape(owners)


def draw_frame_counts(key, part):
    live_count = live_counts(key)
    key = jax.random.fold_in(key, 11)
    upper_bound = jnp.minimum(LMAX, F_DEV // live_count)
    lengths = jax.random.randint(key, (live_count.shape[0], U_CAP), LMIN, upper_bound[:, None] + 1)
    slot_index = jnp.arange(U_CAP, dtype=jnp.int32)[None, :]
    longest = (live_count[:, None] == U_HOME // 4) & (slot_index == 0)
    lengths = jnp.where(longest, LMAX, lengths)
    return jnp.where(slot_index < live_count[:, None], lengths, 0).astype(jnp.int32)


def draw_slot_ids(key, part):
    live_count = live_counts(key)
    key = jax.random.fold_in(key, 23)
    owners = live_count.shape[0]
    grid_rows = owners // N_COL
    first_key, second_key = jax.random.split(key)

    def shuffle_rows(sub_key):
        return jax.random.permutation(sub_key, grid_rows)
    home_order = jax.vmap(shuffle_rows)(jax.random.split(first_key, N_COL))

    def shuffle_home(sub_key):
        return jax.random.permutation(sub_key, U_HOME)
    within = jax.vmap(shuffle_home)(jax.random.split(second_key, owners))
    live_grid = live_count.reshape(grid_rows, N_COL)
    starts = (jnp.cumsum(live_grid, axis=0) - live_grid).reshape(owners)
    owner_col = jnp.arange(owners, dtype=jnp.int32) % N_COL
    slot_index = jnp.arange(U_CAP, dtype=jnp.int32)[None, :]
    global_slot = starts[:, None] + slot_index
    home_row = home_order[owner_col[:, None], global_slot // CAP % grid_rows]
    home_block = home_row * N_COL + owner_col[:, None]
    position = global_slot // (CAP * grid_rows) * CAP + global_slot % CAP
    position = jnp.clip(position, 0, U_HOME - 1)
    utterance = home_block * U_HOME + within[home_block, position]
    return jnp.where(slot_index < live_count[:, None], utterance, N).astype(jnp.int32)


def draw_frames(key, part):
    counts = draw_frame_counts(key, part)
    idents = draw_slot_ids(key, part)
    key = jax.random.fold_in(key, 41)
    owners = counts.shape[0]
    speakers = N // cluster_size
    speaker_key, centre_key, noise_key = jax.random.split(key, 3)
    speaker_of = (jax.random.permutation(speaker_key, N) % speakers).astype(jnp.int32)
    speaker_of = jnp.concatenate([speaker_of, jnp.zeros((1,), jnp.int32)])
    centres = jax.random.normal(centre_key, (speakers, D), jnp.float32)
    spreads = jnp.ones((N + 1,), jnp.float32)
    frame_index = jnp.arange(F_DEV, dtype=jnp.int32)

    def one_owner(owner):
        owner_counts = counts[owner]
        ends = jnp.cumsum(owner_counts)
        finished = (ends[None, :] <= frame_index[:, None]).astype(jnp.int32)
        slot = jnp.minimum(jnp.sum(finished, axis=1), U_CAP - 1)
        utterance = idents[owner][slot]
        live = (frame_index < ends[-1]).astype(jnp.float32)
        speaker = speaker_of[utterance]
        owner_key = jax.random.fold_in(noise_key, owner)
        noise = jax.random.normal(owner_key, (F_DEV, D), jnp.float32)
        centre = centres[speaker] * live[:, None]
        values = 0.6 * centre + 0.8 * spreads[utterance][:, None] * noise
        return jnp.clip(values, -5.0, 5.0).astype(jnp.bfloat16)
    blocks = lax.map(one_owner, jnp.arange(owners, dtype=jnp.int32))
    return blocks.reshape(owners * F_DEV, D)


def draw_plda_weight(key, part):
    key = jax.random.fold_in(key, 53)
    noise = jax.random.normal(key, (E, E), jnp.float32)
    diagonal_part = (jnp.arange(E, dtype=jnp.int32)[:, None] == jnp.arange(E, dtype=jnp.int32)[None, :]).astype(jnp.float32)
    return (diagonal_part + 0.7 / math.sqrt(E) * noise).astype(jnp.bfloat16)


def set_ends(result, key, least, high):
    dims = result.shape
    spot = [jax.random.randint(jax.random.fold_in(key, axis), (), 0, dims[axis]) for axis in range(len(dims))]
    result = result.at[tuple(spot)].set(least)
    longest = dims.index(max(dims))
    spot[longest] = (spot[longest] + 1) % dims[longest]
    return result.at[tuple(spot)].set(high)


def bell_draw(rng, shape, scale, bound, kind=jnp.bfloat16):
    return jnp.clip(scale * jax.random.normal(rng, shape, jnp.float32), -bound, bound).astype(kind)


def setup_inputs(seed: int = 0) -> dict:
    key_list = jax.random.split(jax.random.key(seed), 8)
    return {
        "frames": draw_frames(jax.random.fold_in(key_list[7], 71), 0),
        "frame_counts": draw_frame_counts(jax.random.fold_in(key_list[7], 71), 0),
        "slot_ids": draw_slot_ids(jax.random.fold_in(key_list[7], 71), 0),
        "seed_labels": set_ends(jax.random.randint(key_list[3], (N,), 0, 4 * K), jax.random.fold_in(key_list[3], 1), 0, (4 * K) - 1).astype(jnp.int32),
        "attn_query": bell_draw(key_list[4], (D, HEADS), D ** -0.5, 0.1875),
        "emb_weight": bell_draw(key_list[5], (HEADS * D, E), (HEADS * D) ** -0.5, 0.0625),
        "plda_weight": draw_plda_weight(jax.random.fold_in(key_list[7], 71), 0),
    }


GAIN = 4.0
BETA = 8.0
ALPHA = 0.9
EPSILON = 1e-06

def pool_owner(frames, counts, attn_query, emb_weight):
    ends = jnp.cumsum(counts)
    starts = ends - counts
    frame_index = jnp.arange(frames.shape[0], dtype=jnp.int32)
    member = ((frame_index[None, :] >= starts[:, None]) & (frame_index[None, :] < ends[:, None])).astype(jnp.float32)
    energy = jnp.exp(GAIN * jnp.tanh(jnp.dot(frames, attn_query, preferred_element_type=jnp.float32))).T
    weight_total = jnp.dot(member, energy.T, precision=lax.Precision.HIGHEST)
    weight_total = weight_total + (counts == 0).astype(jnp.float32)[:, None]
    attention = (member[:, None, :] * energy[None, :, :] / weight_total[:, :, None]).astype(jnp.bfloat16)
    attention = attention.reshape(-1, frames.shape[0])
    pooled = jnp.dot(attention, frames, preferred_element_type=jnp.float32).astype(jnp.bfloat16)
    pooled = pooled.reshape(counts.shape[0], -1)
    return jnp.dot(pooled, emb_weight, preferred_element_type=jnp.float32).astype(jnp.bfloat16)

def unit_rows(values):
    return values / jnp.sqrt(lax.optimization_barrier(jnp.mean(values * values, axis=1, keepdims=True)) + EPSILON)

def reference(frames, frame_counts, slot_ids, seed_labels, attn_query, emb_weight, plda_weight):
    owners = frame_counts.shape[0]
    stacked = frames.reshape(owners, -1, frames.shape[1])

    def pool_one(owner_data):
        return pool_owner(owner_data[0], owner_data[1], attn_query, emb_weight)
    embeds = lax.map(pool_one, (stacked, frame_counts))
    flat_ids = slot_ids.reshape(-1)
    embed = jnp.zeros((N, E), jnp.bfloat16).at[flat_ids].set(embeds.reshape(-1, E), mode='drop')
    lengths = jnp.zeros((N,), jnp.float32).at[flat_ids].set(frame_counts.reshape(-1).astype(jnp.float32), mode='drop')
    row_unit = unit_rows(embed.astype(jnp.float32)).astype(jnp.bfloat16)
    projected = jnp.dot(embed, plda_weight, preferred_element_type=jnp.float32)
    col_unit = unit_rows(projected).astype(jnp.bfloat16)
    cosine = jnp.dot(row_unit, col_unit.T, preferred_element_type=jnp.float32) / E
    affinity = ((lengths / FPU)[None, :] * jnp.exp(BETA * cosine)).astype(jnp.bfloat16)
    totals = lax.optimization_barrier(jnp.sum(affinity.astype(jnp.float32), axis=1))
    seeds = (seed_labels[:, None] == jnp.arange(K, dtype=jnp.int32)[None, :]).astype(jnp.float32)
    labels = seeds
    for step_index in range(ITERS):
        label_copy = labels.astype(jnp.bfloat16)
        spread = jnp.dot(affinity, label_copy, preferred_element_type=jnp.float32)
        labels = ALPHA * spread / totals[:, None] + (1.0 - ALPHA) * seeds
    return jnp.log(1.0 + K * labels)
```

```python
import functools

import jax
import jax.numpy as jnp
from jax import lax
from jax.experimental import pallas as pl
from jax.experimental.pallas import tpu as pltpu
from jax.sharding import PartitionSpec as P

MESH = pl.DeviceIdType.MESH
F32 = jnp.float32
BF16 = jnp.bfloat16

D = 1024
HEADS = 8
E = 256
K = 256
FPU = 256
SLOTS = 64
HOME = 32
ROWS = 16
COLS = 8
WIN = 1024
WINDOWS = 8
SEG = 16
ITERS = 3

GAIN = 4.0
BETA = 8.0
ALPHA = 0.9
EPSILON = 1e-06

NT = (((1,), (1,)), ((), ()))
TN = (((0,), (0,)), ((), ()))

PACK, ROWU, COLU, META, TOTS, SUMS, LABS = 0, 1, 2, 3, 4, 5, 8
N_SEMS = 10


def iota(shape, dim):
    return lax.broadcasted_iota(jnp.int32, shape, dim)


def to_column(row, size):
    shape = (size, row.shape[1])
    return jnp.sum(jnp.where(iota(shape, 0) == iota(shape, 1), row, 0.0), axis=1, keepdims=True)


def unit_rows(values):
    return values / jnp.sqrt(jnp.mean(values * values, axis=1, keepdims=True) + EPSILON)


def kernel(
    frames, counts, idents, seeds, query, emb_weight, plda, out,
    frame_buf, weight_buf, segments, packed, inbox, row_units, col_units, metas, meta_own,
    affinity, parts, part_send, part_in, tot_send, tot_in, labels_buf,
    frame_sem, weight_sem, send, recv,
):
    r = lax.axis_index("row")
    c = lax.axis_index("col")
    row_peers = [(lax.rem(r + k, ROWS), c) for k in range(1, ROWS)]
    col_peers = [(r, lax.rem(c + k, COLS)) for k in range(1, COLS)]

    barrier = pltpu.get_barrier_semaphore()
    for peer in row_peers + col_peers:
        pl.semaphore_signal(barrier, inc=1, device_id=peer, device_id_type=MESH)

    def frame_copy(w):
        return pltpu.make_async_copy(
            frames.at[pl.ds(w * WIN, WIN)], frame_buf.at[w], frame_sem.at[w]
        )

    for w in range(WINDOWS):
        frame_copy(w).start()
    weight_copy = pltpu.make_async_copy(emb_weight, weight_buf, weight_sem)
    weight_copy.start()

    live_row = counts[...].astype(F32)
    square = (SLOTS, SLOTS)
    count_square = jnp.broadcast_to(live_row, square)
    ends = jnp.sum(
        jnp.where(iota(square, 1) <= iota(square, 0), count_square, 0.0), axis=1, keepdims=True
    )
    count_col = to_column(live_row, SLOTS)
    starts = ends - count_col
    query_t = query[...].astype(F32).T.astype(BF16)

    def window(w, weight_total):
        frame_copy(w).wait()
        block = frame_buf[w]
        score = lax.dot_general(query_t, block, NT, preferred_element_type=F32)
        energy = jnp.exp(GAIN * jnp.tanh(score))
        first = (w * WIN).astype(F32)
        index = first + iota((SLOTS, WIN), 1).astype(F32)
        past = ends <= index
        rel = jnp.sum(jnp.where(past & (ends > first), 1.0, 0.0), axis=0, keepdims=True)
        member = jnp.where((starts <= index) & (ends > index), 1.0, 0.0).astype(BF16)
        mask = rel == iota((SEG, WIN), 0).astype(F32)
        rows = jnp.concatenate(
            [jnp.where(mask, energy[h : h + 1, :], 0.0) for h in range(HEADS)], axis=0
        ).astype(BF16)
        sums = jnp.dot(rows, block, preferred_element_type=F32)
        for h in range(HEADS):
            segments[h, pl.ds(w * SEG, SEG), :] = sums[h * SEG : (h + 1) * SEG].astype(BF16)
        high = energy.astype(BF16).astype(F32)
        both = jnp.concatenate([high, energy - high], axis=0).astype(BF16)
        return weight_total + lax.dot_general(member, both, NT, preferred_element_type=F32)

    weight_total = lax.fori_loop(0, WINDOWS, window, jnp.zeros((SLOTS, 2 * HEADS), F32))

    wide = (SLOTS, WINDOWS * SEG)
    before = jnp.where(ends <= (iota(wide, 1) // SEG * WIN).astype(F32), 1.0, 0.0)
    target = jnp.sum(before, axis=0, keepdims=True) + (iota((1, WINDOWS * SEG), 1) % SEG).astype(F32)
    gather = jnp.where(target == iota(wide, 0).astype(F32), 1.0, 0.0).astype(BF16)
    dead = jnp.where(count_col > 0.0, 0.0, 1.0)
    weight_copy.wait()
    total = jnp.zeros((SLOTS, E), F32)
    for h in range(HEADS):
        pooled = jnp.dot(gather, segments[h], preferred_element_type=F32)
        scale = weight_total[:, h : h + 1] + weight_total[:, HEADS + h : HEADS + h + 1] + dead
        pooled = (pooled / scale).astype(BF16)
        total = total + jnp.dot(
            pooled, weight_buf[h * D : (h + 1) * D, :], preferred_element_type=F32
        )
    embed = total.astype(BF16)

    ident_row = idents[...]
    dest_row = jnp.where(counts[...] > 0, ident_row // (HOME * COLS), ROWS).astype(F32)
    place_row = (ident_row % HOME).astype(F32)
    dest_col = to_column(dest_row, SLOTS)
    place_col = to_column(place_row, SLOTS)
    same = (dest_col == dest_row) & (iota(square, 0) < iota(square, 1))
    rank_row = jnp.sum(jnp.where(same, 1.0, 0.0), axis=0, keepdims=True)
    spot = dest_row * 16.0 + rank_row
    high_col = jnp.floor(count_col * (1.0 / 256.0))
    lane = iota((SLOTS, 128), 1)
    meta = jnp.where(
        lane == 0,
        place_col + 1.0,
        jnp.where(lane == 1, high_col, jnp.where(lane == 2, count_col - 256.0 * high_col, 0.0)),
    ).astype(BF16)
    place = iota((ROWS * 16, SLOTS), 0).astype(F32)
    letter = jnp.zeros((ROWS * 16, 128), F32)
    for t, part in enumerate((embed[:, :128], embed[:, 128:], meta)):
        pick = jnp.where(place == spot + 4.0 * t, 1.0, 0.0).astype(BF16)
        letter = letter + jnp.dot(pick, part, preferred_element_type=F32)
    packed[...] = letter.astype(BF16)

    pl.semaphore_wait(barrier, ROWS + COLS - 2)
    for peer in row_peers:
        pltpu.make_async_remote_copy(
            packed.at[pl.ds(peer[0] * 16, 16)], inbox.at[pl.ds(r * 16, 16)],
            send.at[PACK], recv.at[PACK], device_id=peer, device_id_type=MESH,
        ).start()
    own = pl.multiple_of(r * 16, 16)
    inbox[pl.ds(own, 16), :] = packed[pl.ds(own, 16), :]
    seed_row = jnp.minimum(seeds[...], K).astype(F32)
    seed_col = to_column(seed_row, HOME)
    seed_hot = jnp.where(seed_col == iota((HOME, K), 1).astype(F32), 1.0, 0.0)

    def wait_bytes(ref, sem):
        pltpu.make_async_copy(ref, ref, sem).wait()

    wait_bytes(inbox.at[pl.ds(0, (ROWS - 1) * 16)], recv.at[PACK])

    got = inbox[...]
    mark = jnp.broadcast_to(got[:, 0:1].astype(F32), (ROWS * 16, 128))
    sub = iota((ROWS * 16, 128), 0) % 16
    lane = iota((ROWS * 16, 128), 1)
    mark = jnp.where(
        sub < 4,
        pltpu.roll(mark, ROWS * 16 - 8, 0),
        jnp.where(sub < 8, pltpu.roll(mark, ROWS * 16 - 4, 0), mark),
    )
    pick = (mark == (lane % HOME + 1).astype(F32)) & (lane // HOME == sub // 4) & (sub < 12)
    home = lax.dot_general(
        jnp.where(pick, 1.0, 0.0).astype(BF16), got, TN, preferred_element_type=F32
    )
    home_embed = jnp.concatenate([home[0:HOME], home[HOME : 2 * HOME]], axis=1)
    unit = unit_rows(home_embed).astype(BF16)
    row_own = pl.multiple_of(c * HOME, HOME)
    col_own = pl.multiple_of(r * HOME, HOME)
    row_units[pl.ds(row_own, HOME), :] = unit
    for peer in col_peers:
        pltpu.make_async_remote_copy(
            row_units.at[pl.ds(row_own, HOME)], row_units.at[pl.ds(row_own, HOME)],
            send.at[ROWU], recv.at[ROWU], device_id=peer, device_id_type=MESH,
        ).start()
    projected = jnp.dot(home_embed.astype(BF16), plda[...], preferred_element_type=F32)
    col_units[pl.ds(col_own, HOME), :] = unit_rows(projected).astype(BF16)
    for peer in row_peers:
        pltpu.make_async_remote_copy(
            col_units.at[pl.ds(col_own, HOME)], col_units.at[pl.ds(col_own, HOME)],
            send.at[COLU], recv.at[COLU], device_id=peer, device_id_type=MESH,
        ).start()
    home_meta = home[2 * HOME : 3 * HOME]
    diagonal = iota((HOME, 128), 0) == iota((HOME, 128), 1) % HOME
    group = iota((HOME, 128), 1) // HOME
    values = jnp.where(
        group == 0, home_meta[:, 1:2], jnp.where(group == 1, home_meta[:, 2:3], seed_col)
    )
    meta_own[0] = jnp.sum(jnp.where(diagonal, values, 0.0), axis=0, keepdims=True)
    metas[r] = meta_own[0]
    for peer in row_peers:
        pltpu.make_async_remote_copy(
            meta_own.at[0], metas.at[r],
            send.at[META], recv.at[META], device_id=peer, device_id_type=MESH,
        ).start()

    wait_bytes(metas.at[pl.ds(0, ROWS - 1)], recv.at[META])
    shape = (128, ROWS * HOME)
    spread_lane = iota(shape, 1) % HOME
    spread_sub = iota(shape, 0)
    take_len = jnp.where(spread_sub == spread_lane, 256.0, 0.0) + jnp.where(
        spread_sub == spread_lane + HOME, 1.0, 0.0
    )
    take_seed = jnp.where(spread_sub == spread_lane + 2 * HOME, 1.0, 0.0)
    meta_rows = jnp.concatenate([metas[k] for k in range(ROWS)], axis=0).astype(BF16)
    mine = iota((ROWS, ROWS * HOME), 0) == iota((ROWS, ROWS * HOME), 1) // HOME

    def column_row(take):
        full = jnp.dot(meta_rows, take.astype(BF16), preferred_element_type=F32)
        return jnp.sum(jnp.where(mine, full, 0.0), axis=0, keepdims=True)

    len_row = column_row(take_len) * (1.0 / FPU)
    seeds_row = column_row(take_seed)
    seeds_t = jnp.where(seeds_row == iota((K, ROWS * HOME), 0).astype(F32), 1.0, 0.0).astype(BF16)

    wait_bytes(row_units.at[pl.ds(0, (COLS - 1) * HOME)], recv.at[ROWU])
    wait_bytes(col_units.at[pl.ds(0, (ROWS - 1) * HOME)], recv.at[COLU])
    cosine = lax.dot_general(row_units[...], col_units[...], NT, preferred_element_type=F32)
    affinity[...] = (len_row * jnp.exp(cosine * (BETA / E))).astype(BF16)

    tot_send[0] = lax.dot_general(
        jnp.ones((8, ROWS * HOME), BF16), affinity[...], NT, preferred_element_type=F32
    )[0:1]
    for k, peer in enumerate(col_peers):
        pltpu.make_async_remote_copy(
            tot_send.at[0], tot_in.at[k],
            send.at[TOTS], recv.at[TOTS], device_id=peer, device_id_type=MESH,
        ).start()

    totals = None
    for step in range(ITERS):
        if step == 0:
            part = lax.dot_general(affinity[...], seeds_t, NT, preferred_element_type=F32)
        else:
            wait_bytes(
                labels_buf.at[step - 1, pl.ds(0, (ROWS - 1) * HOME)], recv.at[LABS + step - 1]
            )
            part = jnp.dot(affinity[...], labels_buf[step - 1], preferred_element_type=F32)
        parts[...] = part
        part_send[step] = part.astype(BF16)
        for k, peer in enumerate(col_peers):
            pltpu.make_async_remote_copy(
                part_send.at[step, pl.ds(peer[1] * HOME, HOME)], part_in.at[step, k],
                send.at[SUMS + step], recv.at[SUMS + step], device_id=peer, device_id_type=MESH,
            ).start()
        if step == 0:
            wait_bytes(tot_in, recv.at[TOTS])
            row_totals = tot_send[0]
            for k in range(COLS - 1):
                row_totals = row_totals + tot_in[k]
            here = iota((HOME, COLS * HOME), 1) == iota((HOME, COLS * HOME), 0) + c * HOME
            totals = jnp.sum(jnp.where(here, row_totals, 0.0), axis=1, keepdims=True)
        wait_bytes(part_in.at[step], recv.at[SUMS + step])
        spread = parts[pl.ds(row_own, HOME), :]
        for k in range(COLS - 1):
            spread = spread + part_in[step, k].astype(F32)
        labels = ALPHA * spread / totals + (1.0 - ALPHA) * seed_hot
        if step < ITERS - 1:
            labels_buf[step, pl.ds(col_own, HOME), :] = labels.astype(BF16)
            for peer in row_peers:
                pltpu.make_async_remote_copy(
                    labels_buf.at[step, pl.ds(col_own, HOME)],
                    labels_buf.at[step, pl.ds(col_own, HOME)],
                    send.at[LABS + step], recv.at[LABS + step], device_id=peer, device_id_type=MESH,
                ).start()
        else:
            out[...] = jnp.log(1.0 + K * labels)

    wait_bytes(packed.at[pl.ds(0, (ROWS - 1) * 16)], send.at[PACK])
    wait_bytes(row_units.at[pl.ds(0, (COLS - 1) * HOME)], send.at[ROWU])
    wait_bytes(col_units.at[pl.ds(0, (ROWS - 1) * HOME)], send.at[COLU])
    wait_bytes(metas.at[pl.ds(0, ROWS - 1)], send.at[META])
    wait_bytes(tot_in, send.at[TOTS])
    for step in range(ITERS):
        wait_bytes(part_in.at[step], send.at[SUMS + step])
    for step in range(ITERS - 1):
        wait_bytes(labels_buf.at[step, pl.ds(0, (ROWS - 1) * HOME)], send.at[LABS + step])


def on_device(frames, frame_counts, slot_ids, seed_labels, attn_query, emb_weight, plda_weight):
    vmem = pl.BlockSpec(memory_space=pltpu.VMEM)
    hbm = pl.BlockSpec(memory_space=pl.ANY)
    return pl.pallas_call(
        kernel,
        name="speaker_linking",
        out_shape=jax.ShapeDtypeStruct((HOME, K), F32),
        in_specs=[hbm, vmem, vmem, vmem, vmem, hbm, vmem],
        out_specs=vmem,
        scratch_shapes=[
            pltpu.VMEM((WINDOWS, WIN, D), BF16),
            pltpu.VMEM((HEADS * D, E), BF16),
            pltpu.VMEM((HEADS, WINDOWS * SEG, D), BF16),
            pltpu.VMEM((ROWS * 16, 128), BF16),
            pltpu.VMEM((ROWS * 16, 128), BF16),
            pltpu.VMEM((COLS * HOME, E), BF16),
            pltpu.VMEM((ROWS * HOME, E), BF16),
            pltpu.VMEM((ROWS, 1, 128), F32),
            pltpu.VMEM((1, 1, 128), F32),
            pltpu.VMEM((COLS * HOME, ROWS * HOME), BF16),
            pltpu.VMEM((COLS * HOME, K), F32),
            pltpu.VMEM((ITERS, COLS * HOME, K), BF16),
            pltpu.VMEM((ITERS, COLS - 1, HOME, K), BF16),
            pltpu.VMEM((1, 1, COLS * HOME), F32),
            pltpu.VMEM((COLS - 1, 1, COLS * HOME), F32),
            pltpu.VMEM((ITERS - 1, ROWS * HOME, K), BF16),
            pltpu.SemaphoreType.DMA((WINDOWS,)),
            pltpu.SemaphoreType.DMA,
            pltpu.SemaphoreType.DMA((N_SEMS,)),
            pltpu.SemaphoreType.DMA((N_SEMS,)),
        ],
        compiler_params=pltpu.CompilerParams(
            collective_id=0, has_side_effects=True, vmem_limit_bytes=48 * 1024 * 1024
        ),
    )(
        frames, frame_counts, slot_ids, seed_labels.reshape(1, HOME), attn_query, emb_weight,
        plda_weight,
    )


def solution(mesh):
    return jax.shard_map(
        on_device,
        mesh=mesh,
        in_specs=(
            P(("row", "col"), None),
            P(("row", "col"), None),
            P(("row", "col"), None),
            P(("row", "col")),
            P(),
            P(),
            P(),
        ),
        out_specs=P(("row", "col"), None),
        check_vma=False,
    )
```

```python
import jax
import jax.numpy as jnp
from jax import lax
from jax.experimental import pallas as pl
from jax.experimental.pallas import tpu as pltpu
from jax.sharding import PartitionSpec as P

MESH = pl.DeviceIdType.MESH
F32 = jnp.float32
BF16 = jnp.bfloat16

D = 1024
HEADS = 8
E = 256
K = 256
FPU = 256
SLOTS = 64
HOME = 32
ROWS = 16
COLS = 8
WIN = 1024
WINDOWS = 8
SEG = 16
SEGS = WINDOWS * SEG
ITERS = 3

GAIN = 4.0
BETA = 8.0
ALPHA = 0.9
EPSILON = 1e-06

NT = (((1,), (1,)), ((), ()))

EARLY, PACK, ROWU, COLU, META, TOTS, SUMS, LABS = 0, 1, 2, 3, 4, 5, 6, 9
N_SEMS = 11


def ring(step):
    return min(step, 4 - step)


ROW_STEPS = sorted(
    [(a, b) for a in range(4) for b in range(4) if a or b], key=lambda s: -ring(s[0]) - ring(s[1])
)
COL_STEPS = sorted([(a, b) for a in range(4) for b in range(2) if a or b], key=lambda s: -ring(s[0]))


def iota(shape, dim):
    return lax.broadcasted_iota(jnp.int32, shape, dim)


def hot(condition):
    return jnp.where(condition, 1.0, 0.0).astype(BF16)


def dot(a, b):
    return jnp.dot(a, b, preferred_element_type=F32)


def to_column(row, size):
    shape = (size, row.shape[1])
    return jnp.sum(jnp.where(iota(shape, 0) == iota(shape, 1), row, 0.0), axis=1, keepdims=True)


def unit_rows(values):
    return values / jnp.sqrt(jnp.mean(values * values, axis=1, keepdims=True) + EPSILON)


def kernel(
    frames, counts_in, idents_in, seeds_in, query_in, emb_weight, plda_in, out,
    counts, idents, seeds, query, plda, frame_buf, weight_buf, segments, seg_totals, projected_segs,
    same_slot, place_hot, early_send, early_in, packed, inbox, row_units, col_units, metas, meta_own,
    affinity, parts, part_send, part_in, tot_send, tot_in, labels_buf,
    small_sem, frame_sem, weight_sem, send, recv,
):
    r = lax.axis_index("row")
    c = lax.axis_index("col")
    row_peers = [
        (lax.rem(r // 4 + a, 4) * 4 + lax.rem(lax.rem(r, 4) + b, 4), c) for a, b in ROW_STEPS
    ]
    col_peers = [
        (r, lax.rem(c // 2 + a, 4) * 2 + lax.rem(lax.rem(c, 2) + b, 2)) for a, b in COL_STEPS
    ]

    def wait_bytes(ref, sem):
        pltpu.make_async_copy(ref, ref, sem).wait()

    def post(src, dst, slot, peer):
        pltpu.make_async_remote_copy(
            src, dst, send.at[slot], recv.at[slot], device_id=peer, device_id_type=MESH
        ).start()

    def frame_copy(w):
        return pltpu.make_async_copy(
            frames.at[pl.ds(w * WIN, WIN)], frame_buf.at[w], frame_sem.at[w]
        )

    small_copies = [
        pltpu.make_async_copy(src, dst, small_sem.at[k])
        for k, (src, dst) in enumerate(
            (
                (counts_in, counts), (idents_in, idents), (query_in, query), (seeds_in, seeds),
                (plda_in, plda),
            )
        )
    ]
    for copy in small_copies[:4]:
        copy.start()
    for w in range(WINDOWS):
        frame_copy(w).start()
    weight_copy = pltpu.make_async_copy(emb_weight, weight_buf, weight_sem)
    weight_copy.start()
    small_copies[4].start()
    barrier = pltpu.get_barrier_semaphore()
    for peer in row_peers + col_peers:
        pl.semaphore_signal(barrier, inc=1, device_id=peer, device_id_type=MESH)
    for copy in small_copies[:4]:
        copy.wait()

    live_row = counts[...].astype(F32)
    square = (SLOTS, SLOTS)
    ends = jnp.sum(
        jnp.where(iota(square, 1) <= iota(square, 0), live_row, 0.0), axis=1, keepdims=True
    )
    count_col = to_column(live_row, SLOTS)
    ident_row = idents[...]
    dest_row = jnp.where(counts[...] > 0, ident_row // (HOME * COLS), ROWS).astype(F32)
    dest_col = to_column(dest_row, SLOTS)
    place_col = to_column((ident_row % HOME).astype(F32), SLOTS)
    rank_col = jnp.sum(
        jnp.where((dest_col == dest_row) & (iota(square, 1) < iota(square, 0)), 1.0, 0.0),
        axis=1, keepdims=True,
    )
    wide = (SLOTS, SEGS)
    before = jnp.where(ends <= (iota(wide, 1) // SEG * WIN).astype(F32), 1.0, 0.0)
    target_row = jnp.sum(before, axis=0, keepdims=True) + (iota((1, SEGS), 1) % SEG).astype(F32)
    same_slot[...] = hot(to_column(target_row, SEGS) == target_row)
    spot = jnp.where(target_row == iota(wide, 0).astype(F32), dest_col * 8.0 + rank_col + 1.0, 0.0)
    spot_row = jnp.sum(spot, axis=0, keepdims=True) - 1.0
    letter_row = iota((SEGS, SEGS), 0)
    place_hot[...] = hot(spot_row == (letter_row // 8 * 8 + letter_row % 4).astype(F32))
    lane = iota((SLOTS, 128), 1)
    mine = (lane // 8 == r) & ((lane % 4).astype(F32) == rank_col)
    high_col = jnp.floor(count_col * (1.0 / 256.0))
    notes = jnp.concatenate(
        [jnp.where(mine, v, 0.0) for v in (place_col + 1.0, high_col, count_col - 256.0 * high_col)],
        axis=1,
    ).astype(BF16)
    notes = dot(hot(dest_row == iota((ROWS, SLOTS), 0).astype(F32)), notes)
    for k in range(ROWS):
        early_send[k] = jnp.concatenate(
            [notes[k : k + 1, :128], 256.0 * notes[k : k + 1, 128:256] + notes[k : k + 1, 256:]],
            axis=1,
        )

    query_t = query[...]

    def score(w):
        frame_copy(w).wait()
        return lax.dot_general(query_t, frame_buf[w], NT, preferred_element_type=F32)

    def pool(w, scores):
        energy = jnp.exp(GAIN * jnp.tanh(scores))
        first = (w * WIN).astype(F32)
        index = first + iota((1, WIN), 1).astype(F32)
        passed = jnp.where((ends <= index) & (ends > first), 1.0, 0.0)
        rel = jnp.sum(passed, axis=0, keepdims=True)
        mask = rel == iota((SEG, WIN), 0).astype(F32)
        rows = jnp.concatenate(
            [jnp.where(mask, energy[h : h + 1, :], 0.0) for h in range(HEADS)], axis=0
        )
        sums = jnp.sum(rows, axis=1, keepdims=True)
        totals = jnp.zeros((SEG, 128), F32)
        for h in range(HEADS):
            totals = jnp.where(iota((SEG, 128), 1) == h, sums[h * SEG : (h + 1) * SEG], totals)
        seg_totals[pl.ds(pl.multiple_of(w * SEG, SEG), SEG), :] = totals
        pooled = dot(rows.astype(BF16), frame_buf[w])
        for h in range(HEADS):
            segments[h, pl.ds(pl.multiple_of(w * SEG, SEG), SEG), :] = pooled[
                h * SEG : (h + 1) * SEG
            ].astype(BF16)

    def two_windows(t, carry):
        first = score(2 * t)
        second = score(2 * t + 1)
        pool(2 * t, first)
        pool(2 * t + 1, second)
        return carry

    lax.fori_loop(0, WINDOWS // 4, two_windows, 0)
    pl.semaphore_wait(barrier, ROWS + COLS - 2)
    for peer in row_peers:
        post(early_send.at[peer[0]], early_in.at[r], EARLY, peer)
    early_in[r] = early_send[r]
    lax.fori_loop(WINDOWS // 4, WINDOWS // 2, two_windows, 0)

    high = seg_totals[...].astype(BF16)
    low = (seg_totals[...] - high.astype(F32)).astype(BF16)
    slot_totals = dot(same_slot[...], high) + dot(same_slot[...], low)
    inverse = jnp.where(slot_totals > 0.0, 1.0 / slot_totals, 0.0)
    weight_copy.wait()
    for h in range(HEADS):
        through = dot(segments[h], weight_buf[h * D : (h + 1) * D, :])
        projected_segs[h * SEGS : (h + 1) * SEGS, :] = (through * inverse[:, h : h + 1]).astype(BF16)
    letters = dot(jnp.concatenate([place_hot[...]] * HEADS, axis=1), projected_segs[...])
    packed[...] = jnp.where(iota((128, 128), 0) % 8 < 4, letters[:, :128], letters[:, 128:])
    for peer in row_peers:
        post(
            packed.at[pl.ds(pl.multiple_of(peer[0] * 8, 8), 8)],
            inbox.at[pl.ds(pl.multiple_of(r * 8, 8), 8)], PACK, peer,
        )
    own = pl.multiple_of(r * 8, 8)
    inbox[pl.ds(own, 8), :] = packed[pl.ds(own, 8), :]

    wait_bytes(early_in.at[pl.ds(0, ROWS - 1)], recv.at[EARLY])
    note = early_in[0]
    for k in range(1, ROWS):
        note = note + early_in[k]
    sub = iota((2 * HOME, 128), 0)
    lane = iota((2 * HOME, 128), 1)
    found = (note[:, :128] == (sub % HOME + 1).astype(F32)) & (lane // 4 % 2 == sub // HOME)
    pick = hot(found)
    home_len = jnp.sum(jnp.where(found, note[:, 128:], 0.0)[:HOME], axis=1, keepdims=True)
    seed_col = to_column(jnp.minimum(seeds[...], K).astype(F32), HOME)
    seed_hot = jnp.where(seed_col == iota((HOME, K), 1).astype(F32), 1.0, 0.0)
    home_high = jnp.floor(home_len * (1.0 / 256.0))
    group = iota((HOME, 128), 1) // HOME
    values = jnp.where(
        group == 0, home_high, jnp.where(group == 1, home_len - 256.0 * home_high, seed_col)
    )
    diagonal = iota((HOME, 128), 0) == iota((HOME, 128), 1) % HOME
    meta_own[0] = jnp.sum(jnp.where(diagonal, values, 0.0), axis=0, keepdims=True)
    metas[r] = meta_own[0]
    for peer in row_peers:
        post(meta_own.at[0], metas.at[r], META, peer)
    small_copies[4].wait()

    row_own = pl.multiple_of(c * HOME, HOME)
    col_own = pl.multiple_of(r * HOME, HOME)
    wait_bytes(inbox.at[pl.ds(0, (ROWS - 1) * 8)], recv.at[PACK])
    halves = dot(pick, inbox[...].astype(BF16))
    home_embed = jnp.concatenate([halves[:HOME], halves[HOME:]], axis=1)
    row_units[pl.ds(row_own, HOME), :] = unit_rows(home_embed).astype(BF16)
    projected = dot(home_embed.astype(BF16), plda[...])
    col_units[pl.ds(col_own, HOME), :] = unit_rows(projected).astype(BF16)
    for peer in row_peers:
        post(
            col_units.at[pl.ds(col_own, HOME)], col_units.at[pl.ds(col_own, HOME)], COLU, peer
        )
    for peer in col_peers:
        post(
            row_units.at[pl.ds(row_own, HOME)], row_units.at[pl.ds(row_own, HOME)], ROWU, peer
        )

    wait_bytes(metas.at[pl.ds(0, ROWS - 1)], recv.at[META])
    shape = (128, ROWS * HOME)
    spread_lane = iota(shape, 1) % HOME
    spread_sub = iota(shape, 0)
    take_len = jnp.where(spread_sub == spread_lane, 256.0, 0.0) + jnp.where(
        spread_sub == spread_lane + HOME, 1.0, 0.0
    )
    take_seed = jnp.where(spread_sub == spread_lane + 2 * HOME, 1.0, 0.0)
    meta_rows = jnp.concatenate([metas[k] for k in range(ROWS)], axis=0).astype(BF16)
    on_row = iota((ROWS, ROWS * HOME), 0) == iota((ROWS, ROWS * HOME), 1) // HOME

    def column_row(take):
        full = dot(meta_rows, take.astype(BF16))
        return jnp.sum(jnp.where(on_row, full, 0.0), axis=0, keepdims=True)

    len_row = column_row(take_len) * (1.0 / FPU)
    seeds_row = column_row(take_seed)
    labels_buf[0] = (
        jnp.where(seeds_row == iota((K, ROWS * HOME), 0).astype(F32), 1.0, 0.0).T.astype(BF16)
    )

    wait_bytes(row_units.at[pl.ds(0, (COLS - 1) * HOME)], recv.at[ROWU])
    wait_bytes(col_units.at[pl.ds(0, (ROWS - 1) * HOME)], recv.at[COLU])
    cosine = lax.dot_general(row_units[...], col_units[...], NT, preferred_element_type=F32)
    affinity[...] = (len_row * jnp.exp(cosine * (BETA / E))).astype(BF16)

    totals = None
    for step in range(ITERS):
        if step > 0:
            wait_bytes(labels_buf.at[step, pl.ds(0, (ROWS - 1) * HOME)], recv.at[LABS + step - 1])
        part = dot(affinity[...], labels_buf[step])
        part_send[step] = part.astype(BF16)
        for k, peer in enumerate(col_peers):
            post(
                part_send.at[step, pl.ds(pl.multiple_of(peer[1] * HOME, HOME), HOME)],
                part_in.at[step, k], SUMS + step, peer,
            )
        parts[...] = part
        if step == 0:
            tot_send[0] = lax.dot_general(
                jnp.ones((8, ROWS * HOME), BF16), affinity[...], NT, preferred_element_type=F32
            )[0:1]
            for k, peer in enumerate(col_peers):
                post(tot_send.at[0], tot_in.at[k], TOTS, peer)
            wait_bytes(tot_in, recv.at[TOTS])
            row_totals = tot_send[0]
            for k in range(COLS - 1):
                row_totals = row_totals + tot_in[k]
            here = iota((HOME, COLS * HOME), 1) == iota((HOME, COLS * HOME), 0) + c * HOME
            totals = jnp.sum(jnp.where(here, row_totals, 0.0), axis=1, keepdims=True)
        wait_bytes(part_in.at[step], recv.at[SUMS + step])
        spread = parts[pl.ds(row_own, HOME), :]
        for k in range(COLS - 1):
            spread = spread + part_in[step, k].astype(F32)
        labels = ALPHA * spread / totals + (1.0 - ALPHA) * seed_hot
        if step < ITERS - 1:
            labels_buf[step + 1, pl.ds(col_own, HOME), :] = labels.astype(BF16)
            for peer in row_peers:
                post(
                    labels_buf.at[step + 1, pl.ds(col_own, HOME)],
                    labels_buf.at[step + 1, pl.ds(col_own, HOME)], LABS + step, peer,
                )
        else:
            out[...] = jnp.log(1.0 + K * labels)

    wait_bytes(early_in.at[pl.ds(0, ROWS - 1)], send.at[EARLY])
    wait_bytes(inbox.at[pl.ds(0, (ROWS - 1) * 8)], send.at[PACK])
    wait_bytes(row_units.at[pl.ds(0, (COLS - 1) * HOME)], send.at[ROWU])
    wait_bytes(col_units.at[pl.ds(0, (ROWS - 1) * HOME)], send.at[COLU])
    wait_bytes(metas.at[pl.ds(0, ROWS - 1)], send.at[META])
    wait_bytes(tot_in, send.at[TOTS])
    for step in range(ITERS):
        wait_bytes(part_in.at[step], send.at[SUMS + step])
    for step in range(ITERS - 1):
        wait_bytes(labels_buf.at[step + 1, pl.ds(0, (ROWS - 1) * HOME)], send.at[LABS + step])


def on_device(frames, frame_counts, slot_ids, seed_labels, attn_query, emb_weight, plda_weight):
    vmem = pl.BlockSpec(memory_space=pltpu.VMEM)
    hbm = pl.BlockSpec(memory_space=pl.ANY)
    return pl.pallas_call(
        kernel,
        name="speaker_linking",
        out_shape=jax.ShapeDtypeStruct((HOME, K), F32),
        in_specs=[hbm] * 7,
        out_specs=vmem,
        scratch_shapes=[
            pltpu.VMEM((1, SLOTS), jnp.int32),
            pltpu.VMEM((1, SLOTS), jnp.int32),
            pltpu.VMEM((1, HOME), jnp.int32),
            pltpu.VMEM((HEADS, D), BF16),
            pltpu.VMEM((E, E), BF16),
            pltpu.VMEM((WINDOWS, WIN, D), BF16),
            pltpu.VMEM((HEADS * D, E), BF16),
            pltpu.VMEM((HEADS, SEGS, D), BF16),
            pltpu.VMEM((SEGS, 128), F32),
            pltpu.VMEM((HEADS * SEGS, E), BF16),
            pltpu.VMEM((SEGS, SEGS), BF16),
            pltpu.VMEM((SEGS, SEGS), BF16),
            pltpu.VMEM((ROWS, 1, 256), F32),
            pltpu.VMEM((ROWS, 1, 256), F32),
            pltpu.VMEM((ROWS * 8, 128), F32),
            pltpu.VMEM((ROWS * 8, 128), F32),
            pltpu.VMEM((COLS * HOME, E), BF16),
            pltpu.VMEM((ROWS * HOME, E), BF16),
            pltpu.VMEM((ROWS, 1, 128), F32),
            pltpu.VMEM((1, 1, 128), F32),
            pltpu.VMEM((COLS * HOME, ROWS * HOME), BF16),
            pltpu.VMEM((COLS * HOME, K), F32),
            pltpu.VMEM((ITERS, COLS * HOME, K), BF16),
            pltpu.VMEM((ITERS, COLS - 1, HOME, K), BF16),
            pltpu.VMEM((1, 1, COLS * HOME), F32),
            pltpu.VMEM((COLS - 1, 1, COLS * HOME), F32),
            pltpu.VMEM((ITERS, ROWS * HOME, K), BF16),
            pltpu.SemaphoreType.DMA((5,)),
            pltpu.SemaphoreType.DMA((WINDOWS,)),
            pltpu.SemaphoreType.DMA,
            pltpu.SemaphoreType.DMA((N_SEMS,)),
            pltpu.SemaphoreType.DMA((N_SEMS,)),
        ],
        compiler_params=pltpu.CompilerParams(
            collective_id=0, has_side_effects=True, vmem_limit_bytes=60 * 1024 * 1024
        ),
    )(
        frames, frame_counts, slot_ids, seed_labels.reshape(1, HOME), attn_query.T, emb_weight,
        plda_weight,
    )


def solution(mesh):
    return jax.shard_map(
        on_device,
        mesh=mesh,
        in_specs=(
            P(("row", "col"), None),
            P(("row", "col"), None),
            P(("row", "col"), None),
            P(("row", "col")),
            P(),
            P(),
            P(),
        ),
        out_specs=P(("row", "col"), None),
        check_vma=False,
    )
```

```python
import jax
import jax.numpy as jnp
from jax import lax
from jax.experimental import pallas as pl
from jax.experimental.pallas import tpu as pltpu
from jax.sharding import PartitionSpec as P

MESH = pl.DeviceIdType.MESH
F32 = jnp.float32
BF16 = jnp.bfloat16

D = 1024
HEADS = 8
E = 256
K = 256
FPU = 256
SLOTS = 64
HOME = 32
ROWS = 16
COLS = 8
WIN = 1024
WINDOWS = 8
SEG = 16
SEGS = WINDOWS * SEG
ITERS = 3

GAIN = 4.0
BETA = 8.0
ALPHA = 0.9
EPSILON = 1e-06

NT = (((1,), (1,)), ((), ()))

EARLY, PACK, ROWU, COLU, META, TOTS, SUMS, LABS = 0, 1, 2, 3, 4, 5, 6, 9
N_SEMS = 11


def ring(step):
    return min(step, 4 - step)


ROW_STEPS = sorted(
    [(a, b) for a in range(4) for b in range(4) if a or b], key=lambda s: -ring(s[0]) - ring(s[1])
)
COL_STEPS = sorted([(a, b) for a in range(4) for b in range(2) if a or b], key=lambda s: -ring(s[0]))


def iota(shape, dim):
    return lax.broadcasted_iota(jnp.int32, shape, dim)


def hot(condition):
    return jnp.where(condition, 1.0, 0.0).astype(BF16)


def dot(a, b):
    return jnp.dot(a, b, preferred_element_type=F32)


def to_column(row, size):
    shape = (size, row.shape[1])
    return jnp.sum(jnp.where(iota(shape, 0) == iota(shape, 1), row, 0.0), axis=1, keepdims=True)


def unit_rows(values):
    return values / jnp.sqrt(jnp.mean(values * values, axis=1, keepdims=True) + EPSILON)


def kernel(
    frames, counts_in, idents_in, seeds_in, query_in, emb_weight, plda_in, out,
    counts, idents, seeds, query, plda, frame_buf, weight_buf, segments, seg_totals, projected_segs,
    same_slot, place_hot, early_send, early_in, packed, inbox, row_units, col_units, metas, meta_own,
    affinity, parts, part_send, part_in, tot_send, tot_in, labels_buf,
    small_sem, frame_sem, weight_sem, send, recv,
):
    r = lax.axis_index("row")
    c = lax.axis_index("col")
    row_peers = [
        (lax.rem(r // 4 + a, 4) * 4 + lax.rem(lax.rem(r, 4) + b, 4), c) for a, b in ROW_STEPS
    ]
    col_peers = [
        (r, lax.rem(c // 2 + a, 4) * 2 + lax.rem(lax.rem(c, 2) + b, 2)) for a, b in COL_STEPS
    ]

    def wait_bytes(ref, sem):
        pltpu.make_async_copy(ref, ref, sem).wait()

    def post(src, dst, slot, peer):
        pltpu.make_async_remote_copy(
            src, dst, send.at[slot], recv.at[slot], device_id=peer, device_id_type=MESH
        ).start()

    def frame_copy(w):
        return pltpu.make_async_copy(
            frames.at[pl.ds(w * WIN, WIN)], frame_buf.at[w], frame_sem.at[w]
        )

    small_copies = [
        pltpu.make_async_copy(src, dst, small_sem.at[k])
        for k, (src, dst) in enumerate(
            (
                (counts_in, counts), (idents_in, idents), (query_in, query), (seeds_in, seeds),
                (plda_in, plda),
            )
        )
    ]
    for copy in small_copies[:4]:
        copy.start()
    for w in range(2):
        frame_copy(w).start()
    barrier = pltpu.get_barrier_semaphore()
    for peer in row_peers + col_peers:
        pl.semaphore_signal(barrier, inc=1, device_id=peer, device_id_type=MESH)
    for copy in small_copies[:4]:
        copy.wait()
    for w in range(2, WINDOWS):
        frame_copy(w).start()
    weight_copy = pltpu.make_async_copy(emb_weight, weight_buf, weight_sem)
    weight_copy.start()
    small_copies[4].start()

    live_row = counts[...].astype(F32)
    square = (SLOTS, SLOTS)
    ends = jnp.sum(
        jnp.where(iota(square, 1) <= iota(square, 0), live_row, 0.0), axis=1, keepdims=True
    )
    count_col = to_column(live_row, SLOTS)
    ident_row = idents[...]
    dest_row = jnp.where(counts[...] > 0, ident_row // (HOME * COLS), ROWS).astype(F32)
    dest_col = to_column(dest_row, SLOTS)
    place_col = to_column((ident_row % HOME).astype(F32), SLOTS)
    rank_col = jnp.sum(
        jnp.where((dest_col == dest_row) & (iota(square, 1) < iota(square, 0)), 1.0, 0.0),
        axis=1, keepdims=True,
    )
    wide = (SLOTS, SEGS)
    before = jnp.where(ends <= (iota(wide, 1) // SEG * WIN).astype(F32), 1.0, 0.0)
    target_row = jnp.sum(before, axis=0, keepdims=True) + (iota((1, SEGS), 1) % SEG).astype(F32)
    same_slot[...] = hot(to_column(target_row, SEGS) == target_row)
    spot = jnp.where(target_row == iota(wide, 0).astype(F32), dest_col * 8.0 + rank_col + 1.0, 0.0)
    spot_row = jnp.sum(spot, axis=0, keepdims=True) - 1.0
    letter_row = iota((SEGS, SEGS), 0)
    place_hot[...] = hot(spot_row == (letter_row // 8 * 8 + letter_row % 4).astype(F32))
    lane = iota((SLOTS, 128), 1)
    mine = (lane // 8 == r) & ((lane % 4).astype(F32) == rank_col)
    high_col = jnp.floor(count_col * (1.0 / 256.0))
    notes = jnp.concatenate(
        [jnp.where(mine, v, 0.0) for v in (place_col + 1.0, high_col, count_col - 256.0 * high_col)],
        axis=1,
    ).astype(BF16)
    notes = dot(hot(dest_row == iota((ROWS, SLOTS), 0).astype(F32)), notes)
    for k in range(ROWS):
        early_send[k] = jnp.concatenate(
            [notes[k : k + 1, :128], 256.0 * notes[k : k + 1, 128:256] + notes[k : k + 1, 256:]],
            axis=1,
        )

    query_t = query[...]

    def score(w):
        frame_copy(w).wait()
        return lax.dot_general(query_t, frame_buf[w], NT, preferred_element_type=F32)

    def pool(w, scores):
        energy = jnp.exp(GAIN * jnp.tanh(scores))
        first = (w * WIN).astype(F32)
        index = first + iota((1, WIN), 1).astype(F32)
        passed = jnp.where((ends <= index) & (ends > first), 1.0, 0.0)
        rel = jnp.sum(passed, axis=0, keepdims=True)
        mask = rel == iota((SEG, WIN), 0).astype(F32)
        rows = jnp.concatenate(
            [jnp.where(mask, energy[h : h + 1, :], 0.0) for h in range(HEADS)], axis=0
        )
        sums = jnp.sum(rows, axis=1, keepdims=True)
        totals = jnp.zeros((SEG, 128), F32)
        for h in range(HEADS):
            totals = jnp.where(iota((SEG, 128), 1) == h, sums[h * SEG : (h + 1) * SEG], totals)
        seg_totals[pl.ds(pl.multiple_of(w * SEG, SEG), SEG), :] = totals
        pooled = dot(rows.astype(BF16), frame_buf[w])
        for h in range(HEADS):
            segments[h, pl.ds(pl.multiple_of(w * SEG, SEG), SEG), :] = pooled[
                h * SEG : (h + 1) * SEG
            ].astype(BF16)

    def two_windows(t, carry):
        first = score(2 * t)
        second = score(2 * t + 1)
        pool(2 * t, first)
        pool(2 * t + 1, second)
        return carry

    lax.fori_loop(0, WINDOWS // 4, two_windows, 0)
    pl.semaphore_wait(barrier, ROWS + COLS - 2)
    for peer in row_peers:
        post(early_send.at[peer[0]], early_in.at[r], EARLY, peer)
    early_in[r] = early_send[r]
    lax.fori_loop(WINDOWS // 4, WINDOWS // 2, two_windows, 0)

    high = seg_totals[...].astype(BF16)
    low = (seg_totals[...] - high.astype(F32)).astype(BF16)
    slot_totals = dot(same_slot[...], high) + dot(same_slot[...], low)
    inverse = jnp.where(slot_totals > 0.0, 1.0 / slot_totals, 0.0)
    weight_copy.wait()
    for h in range(HEADS):
        through = dot(segments[h], weight_buf[h * D : (h + 1) * D, :])
        projected_segs[h * SEGS : (h + 1) * SEGS, :] = (through * inverse[:, h : h + 1]).astype(BF16)
    letters = dot(jnp.concatenate([place_hot[...]] * HEADS, axis=1), projected_segs[...])
    packed[...] = jnp.where(iota((128, 128), 0) % 8 < 4, letters[:, :128], letters[:, 128:])
    for peer in row_peers:
        post(
            packed.at[pl.ds(pl.multiple_of(peer[0] * 8, 8), 8)],
            inbox.at[pl.ds(pl.multiple_of(r * 8, 8), 8)], PACK, peer,
        )
    own = pl.multiple_of(r * 8, 8)
    inbox[pl.ds(own, 8), :] = packed[pl.ds(own, 8), :]

    wait_bytes(early_in.at[pl.ds(0, ROWS - 1)], recv.at[EARLY])
    note = early_in[0]
    for k in range(1, ROWS):
        note = note + early_in[k]
    sub = iota((2 * HOME, 128), 0)
    lane = iota((2 * HOME, 128), 1)
    found = (note[:, :128] == (sub % HOME + 1).astype(F32)) & (lane // 4 % 2 == sub // HOME)
    pick = hot(found)
    home_len = jnp.sum(jnp.where(found, note[:, 128:], 0.0)[:HOME], axis=1, keepdims=True)
    seed_col = to_column(jnp.minimum(seeds[...], K).astype(F32), HOME)
    seed_hot = jnp.where(seed_col == iota((HOME, K), 1).astype(F32), 1.0, 0.0)
    home_high = jnp.floor(home_len * (1.0 / 256.0))
    group = iota((HOME, 128), 1) // HOME
    values = jnp.where(
        group == 0, home_high, jnp.where(group == 1, home_len - 256.0 * home_high, seed_col)
    )
    diagonal = iota((HOME, 128), 0) == iota((HOME, 128), 1) % HOME
    meta_own[0] = jnp.sum(jnp.where(diagonal, values, 0.0), axis=0, keepdims=True)
    metas[r] = meta_own[0]
    for peer in row_peers:
        post(meta_own.at[0], metas.at[r], META, peer)
    small_copies[4].wait()

    row_own = pl.multiple_of(c * HOME, HOME)
    col_own = pl.multiple_of(r * HOME, HOME)
    wait_bytes(inbox.at[pl.ds(0, (ROWS - 1) * 8)], recv.at[PACK])
    halves = dot(pick, inbox[...].astype(BF16))
    home_embed = jnp.concatenate([halves[:HOME], halves[HOME:]], axis=1)
    row_units[pl.ds(row_own, HOME), :] = unit_rows(home_embed).astype(BF16)
    projected = dot(home_embed.astype(BF16), plda[...])
    col_units[pl.ds(col_own, HOME), :] = unit_rows(projected).astype(BF16)
    for peer in row_peers:
        post(
            col_units.at[pl.ds(col_own, HOME)], col_units.at[pl.ds(col_own, HOME)], COLU, peer
        )
    for peer in col_peers:
        post(
            row_units.at[pl.ds(row_own, HOME)], row_units.at[pl.ds(row_own, HOME)], ROWU, peer
        )

    wait_bytes(metas.at[pl.ds(0, ROWS - 1)], recv.at[META])
    shape = (128, ROWS * HOME)
    spread_lane = iota(shape, 1) % HOME
    spread_sub = iota(shape, 0)
    take_len = jnp.where(spread_sub == spread_lane, 256.0, 0.0) + jnp.where(
        spread_sub == spread_lane + HOME, 1.0, 0.0
    )
    take_seed = jnp.where(spread_sub == spread_lane + 2 * HOME, 1.0, 0.0)
    meta_rows = jnp.concatenate([metas[k] for k in range(ROWS)], axis=0).astype(BF16)
    on_row = iota((ROWS, ROWS * HOME), 0) == iota((ROWS, ROWS * HOME), 1) // HOME

    def column_row(take):
        full = dot(meta_rows, take.astype(BF16))
        return jnp.sum(jnp.where(on_row, full, 0.0), axis=0, keepdims=True)

    len_row = column_row(take_len) * (1.0 / FPU)
    seeds_row = column_row(take_seed)
    labels_buf[0] = (
        jnp.where(seeds_row == iota((K, ROWS * HOME), 0).astype(F32), 1.0, 0.0).T.astype(BF16)
    )

    wait_bytes(row_units.at[pl.ds(0, (COLS - 1) * HOME)], recv.at[ROWU])
    wait_bytes(col_units.at[pl.ds(0, (ROWS - 1) * HOME)], recv.at[COLU])
    cosine = lax.dot_general(row_units[...], col_units[...], NT, preferred_element_type=F32)
    affinity[...] = (len_row * jnp.exp(cosine * (BETA / E))).astype(BF16)

    totals = None
    for step in range(ITERS):
        if step > 0:
            wait_bytes(labels_buf.at[step, pl.ds(0, (ROWS - 1) * HOME)], recv.at[LABS + step - 1])
        part = dot(affinity[...], labels_buf[step])
        part_send[step] = part.astype(BF16)
        for k, peer in enumerate(col_peers):
            post(
                part_send.at[step, pl.ds(pl.multiple_of(peer[1] * HOME, HOME), HOME)],
                part_in.at[step, k], SUMS + step, peer,
            )
        parts[...] = part
        if step == 0:
            tot_send[0] = lax.dot_general(
                jnp.ones((8, ROWS * HOME), BF16), affinity[...], NT, preferred_element_type=F32
            )[0:1]
            for k, peer in enumerate(col_peers):
                post(tot_send.at[0], tot_in.at[k], TOTS, peer)
            wait_bytes(tot_in, recv.at[TOTS])
            row_totals = tot_send[0]
            for k in range(COLS - 1):
                row_totals = row_totals + tot_in[k]
            here = iota((HOME, COLS * HOME), 1) == iota((HOME, COLS * HOME), 0) + c * HOME
            totals = jnp.sum(jnp.where(here, row_totals, 0.0), axis=1, keepdims=True)
        wait_bytes(part_in.at[step], recv.at[SUMS + step])
        spread = parts[pl.ds(row_own, HOME), :]
        for k in range(COLS - 1):
            spread = spread + part_in[step, k].astype(F32)
        labels = ALPHA * spread / totals + (1.0 - ALPHA) * seed_hot
        if step < ITERS - 1:
            labels_buf[step + 1, pl.ds(col_own, HOME), :] = labels.astype(BF16)
            for peer in row_peers:
                post(
                    labels_buf.at[step + 1, pl.ds(col_own, HOME)],
                    labels_buf.at[step + 1, pl.ds(col_own, HOME)], LABS + step, peer,
                )
        else:
            out[...] = jnp.log(1.0 + K * labels)

    wait_bytes(early_in.at[pl.ds(0, ROWS - 1)], send.at[EARLY])
    wait_bytes(inbox.at[pl.ds(0, (ROWS - 1) * 8)], send.at[PACK])
    wait_bytes(row_units.at[pl.ds(0, (COLS - 1) * HOME)], send.at[ROWU])
    wait_bytes(col_units.at[pl.ds(0, (ROWS - 1) * HOME)], send.at[COLU])
    wait_bytes(metas.at[pl.ds(0, ROWS - 1)], send.at[META])
    wait_bytes(tot_in, send.at[TOTS])
    for step in range(ITERS):
        wait_bytes(part_in.at[step], send.at[SUMS + step])
    for step in range(ITERS - 1):
        wait_bytes(labels_buf.at[step + 1, pl.ds(0, (ROWS - 1) * HOME)], send.at[LABS + step])


def on_device(frames, frame_counts, slot_ids, seed_labels, attn_query, emb_weight, plda_weight):
    vmem = pl.BlockSpec(memory_space=pltpu.VMEM)
    hbm = pl.BlockSpec(memory_space=pl.ANY)
    return pl.pallas_call(
        kernel,
        name="speaker_linking",
        out_shape=jax.ShapeDtypeStruct((HOME, K), F32),
        in_specs=[hbm] * 7,
        out_specs=vmem,
        scratch_shapes=[
            pltpu.VMEM((1, SLOTS), jnp.int32),
            pltpu.VMEM((1, SLOTS), jnp.int32),
            pltpu.VMEM((1, HOME), jnp.int32),
            pltpu.VMEM((HEADS, D), BF16),
            pltpu.VMEM((E, E), BF16),
            pltpu.VMEM((WINDOWS, WIN, D), BF16),
            pltpu.VMEM((HEADS * D, E), BF16),
            pltpu.VMEM((HEADS, SEGS, D), BF16),
            pltpu.VMEM((SEGS, 128), F32),
            pltpu.VMEM((HEADS * SEGS, E), BF16),
            pltpu.VMEM((SEGS, SEGS), BF16),
            pltpu.VMEM((SEGS, SEGS), BF16),
            pltpu.VMEM((ROWS, 1, 256), F32),
            pltpu.VMEM((ROWS, 1, 256), F32),
            pltpu.VMEM((ROWS * 8, 128), F32),
            pltpu.VMEM((ROWS * 8, 128), F32),
            pltpu.VMEM((COLS * HOME, E), BF16),
            pltpu.VMEM((ROWS * HOME, E), BF16),
            pltpu.VMEM((ROWS, 1, 128), F32),
            pltpu.VMEM((1, 1, 128), F32),
            pltpu.VMEM((COLS * HOME, ROWS * HOME), BF16),
            pltpu.VMEM((COLS * HOME, K), F32),
            pltpu.VMEM((ITERS, COLS * HOME, K), BF16),
            pltpu.VMEM((ITERS, COLS - 1, HOME, K), BF16),
            pltpu.VMEM((1, 1, COLS * HOME), F32),
            pltpu.VMEM((COLS - 1, 1, COLS * HOME), F32),
            pltpu.VMEM((ITERS, ROWS * HOME, K), BF16),
            pltpu.SemaphoreType.DMA((5,)),
            pltpu.SemaphoreType.DMA((WINDOWS,)),
            pltpu.SemaphoreType.DMA,
            pltpu.SemaphoreType.DMA((N_SEMS,)),
            pltpu.SemaphoreType.DMA((N_SEMS,)),
        ],
        compiler_params=pltpu.CompilerParams(
            collective_id=0, has_side_effects=True, vmem_limit_bytes=60 * 1024 * 1024
        ),
    )(
        frames, frame_counts, slot_ids, seed_labels.reshape(1, HOME), attn_query.T, emb_weight,
        plda_weight,
    )


def solution(mesh):
    return jax.shard_map(
        on_device,
        mesh=mesh,
        in_specs=(
            P(("row", "col"), None),
            P(("row", "col"), None),
            P(("row", "col"), None),
            P(("row", "col")),
            P(),
            P(),
            P(),
        ),
        out_specs=P(("row", "col"), None),
        check_vma=False,
    )
```

```python
import jax
import jax.numpy as jnp
from jax import lax
from jax.experimental import pallas as pl
from jax.experimental.pallas import tpu as pltpu
from jax.sharding import PartitionSpec as P

MESH = pl.DeviceIdType.MESH
F32 = jnp.float32
BF16 = jnp.bfloat16

D = 1024
HEADS = 8
E = 256
K = 256
FPU = 256
SLOTS = 64
HOME = 32
ROWS = 16
COLS = 8
WIN = 1024
WINDOWS = 8
SEG = 16
SEGS = WINDOWS * SEG
ITERS = 3
HALF = 128

GAIN = 4.0
BETA = 8.0
ALPHA = 0.9
EPSILON = 1e-06

NT = (((1,), (1,)), ((), ()))

EARLY, PACK, ROWU, COLU, META, TOTS, SUMS, LABS = 0, 1, 2, 3, 4, 5, 6, 12
N_SEMS = 16


def ring(step):
    return min(step, 4 - step)


ROW_STEPS = sorted(
    [(a, b) for a in range(4) for b in range(4) if a or b], key=lambda s: -ring(s[0]) - ring(s[1])
)
COL_STEPS = sorted([(a, b) for a in range(4) for b in range(2) if a or b], key=lambda s: -ring(s[0]))


def iota(shape, dim):
    return lax.broadcasted_iota(jnp.int32, shape, dim)


def hot(condition):
    return jnp.where(condition, 1.0, 0.0).astype(BF16)


def dot(a, b):
    return jnp.dot(a, b, preferred_element_type=F32)


def to_column(row, size):
    shape = (size, row.shape[1])
    return jnp.sum(jnp.where(iota(shape, 0) == iota(shape, 1), row, 0.0), axis=1, keepdims=True)


def unit_rows(values):
    return values / jnp.sqrt(jnp.mean(values * values, axis=1, keepdims=True) + EPSILON)


def kernel(
    frames, counts_in, idents_in, seeds_in, query_in, emb_weight, plda_in, out,
    counts, idents, seeds, query, plda, frame_buf, weight_buf, segments, seg_totals, projected_segs,
    same_slot, place_hot, early_send, early_in, packed, inbox, row_units, col_units, metas, meta_own,
    affinity, parts, part_send, part_in, tot_send, tot_in, labels_buf,
    small_sem, frame_sem, weight_sem, send, recv,
):
    r = lax.axis_index("row")
    c = lax.axis_index("col")
    row_peers = [
        (lax.rem(r // 4 + a, 4) * 4 + lax.rem(lax.rem(r, 4) + b, 4), c) for a, b in ROW_STEPS
    ]
    col_peers = [
        (r, lax.rem(c // 2 + a, 4) * 2 + lax.rem(lax.rem(c, 2) + b, 2)) for a, b in COL_STEPS
    ]

    def wait_bytes(ref, sem):
        pltpu.make_async_copy(ref, ref, sem).wait()

    def post(src, dst, slot, peer):
        pltpu.make_async_remote_copy(
            src, dst, send.at[slot], recv.at[slot], device_id=peer, device_id_type=MESH
        ).start()

    def frame_copy(w):
        return pltpu.make_async_copy(
            frames.at[pl.ds(w * WIN, WIN)], frame_buf.at[w], frame_sem.at[w]
        )

    small_copies = [
        pltpu.make_async_copy(src, dst, small_sem.at[k])
        for k, (src, dst) in enumerate(
            (
                (counts_in, counts), (idents_in, idents), (query_in, query), (seeds_in, seeds),
                (plda_in, plda),
            )
        )
    ]
    for copy in small_copies[:4]:
        copy.start()
    for w in range(2):
        frame_copy(w).start()
    barrier = pltpu.get_barrier_semaphore()
    for peer in row_peers + col_peers:
        pl.semaphore_signal(barrier, inc=1, device_id=peer, device_id_type=MESH)
    for copy in small_copies[:4]:
        copy.wait()
    for w in range(2, WINDOWS):
        frame_copy(w).start()
    weight_copy = pltpu.make_async_copy(emb_weight, weight_buf, weight_sem)
    weight_copy.start()
    small_copies[4].start()

    live_row = counts[...].astype(F32)
    square = (SLOTS, SLOTS)
    ends = jnp.sum(
        jnp.where(iota(square, 1) <= iota(square, 0), live_row, 0.0), axis=1, keepdims=True
    )
    count_col = to_column(live_row, SLOTS)
    ident_row = idents[...]
    dest_row = jnp.where(counts[...] > 0, ident_row // (HOME * COLS), ROWS).astype(F32)
    dest_col = to_column(dest_row, SLOTS)
    place_col = to_column((ident_row % HOME).astype(F32), SLOTS)
    rank_col = jnp.sum(
        jnp.where((dest_col == dest_row) & (iota(square, 1) < iota(square, 0)), 1.0, 0.0),
        axis=1, keepdims=True,
    )
    wide = (SLOTS, SEGS)
    before = jnp.where(ends <= (iota(wide, 1) // SEG * WIN).astype(F32), 1.0, 0.0)
    target_row = jnp.sum(before, axis=0, keepdims=True) + (iota((1, SEGS), 1) % SEG).astype(F32)
    same_slot[...] = hot(to_column(target_row, SEGS) == target_row)
    spot = jnp.where(target_row == iota(wide, 0).astype(F32), dest_col * 8.0 + rank_col + 1.0, 0.0)
    spot_row = jnp.sum(spot, axis=0, keepdims=True) - 1.0
    letter_row = iota((SEGS, SEGS), 0)
    place_hot[...] = hot(spot_row == (letter_row // 8 * 8 + letter_row % 4).astype(F32))
    lane = iota((SLOTS, 128), 1)
    mine = (lane // 8 == r) & ((lane % 4).astype(F32) == rank_col)
    high_col = jnp.floor(count_col * (1.0 / 256.0))
    notes = jnp.concatenate(
        [jnp.where(mine, v, 0.0) for v in (place_col + 1.0, high_col, count_col - 256.0 * high_col)],
        axis=1,
    ).astype(BF16)
    notes = dot(hot(dest_row == iota((ROWS, SLOTS), 0).astype(F32)), notes)
    for k in range(ROWS):
        early_send[k] = jnp.concatenate(
            [notes[k : k + 1, :128], 256.0 * notes[k : k + 1, 128:256] + notes[k : k + 1, 256:]],
            axis=1,
        )

    query_t = query[...]

    def score(w):
        frame_copy(w).wait()
        return lax.dot_general(query_t, frame_buf[w], NT, preferred_element_type=F32)

    def pool(w, scores):
        energy = jnp.exp(GAIN * jnp.tanh(scores))
        first = (w * WIN).astype(F32)
        index = first + iota((1, WIN), 1).astype(F32)
        passed = jnp.where((ends <= index) & (ends > first), 1.0, 0.0)
        rel = jnp.sum(passed, axis=0, keepdims=True)
        mask = rel == iota((SEG, WIN), 0).astype(F32)
        rows = jnp.concatenate(
            [jnp.where(mask, energy[h : h + 1, :], 0.0) for h in range(HEADS)], axis=0
        )
        sums = jnp.sum(rows, axis=1, keepdims=True)
        totals = jnp.zeros((SEG, 128), F32)
        for h in range(HEADS):
            totals = jnp.where(iota((SEG, 128), 1) == h, sums[h * SEG : (h + 1) * SEG], totals)
        seg_totals[pl.ds(pl.multiple_of(w * SEG, SEG), SEG), :] = totals
        pooled = dot(rows.astype(BF16), frame_buf[w])
        for h in range(HEADS):
            segments[h, pl.ds(pl.multiple_of(w * SEG, SEG), SEG), :] = pooled[
                h * SEG : (h + 1) * SEG
            ].astype(BF16)

    def two_windows(t, carry):
        first = score(2 * t)
        second = score(2 * t + 1)
        pool(2 * t, first)
        pool(2 * t + 1, second)
        return carry

    lax.fori_loop(0, WINDOWS // 4, two_windows, 0)
    pl.semaphore_wait(barrier, ROWS + COLS - 2)
    for peer in row_peers:
        post(early_send.at[peer[0]], early_in.at[r], EARLY, peer)
    early_in[r] = early_send[r]
    lax.fori_loop(WINDOWS // 4, WINDOWS // 2, two_windows, 0)

    high = seg_totals[...].astype(BF16)
    low = (seg_totals[...] - high.astype(F32)).astype(BF16)
    slot_totals = dot(same_slot[...], high) + dot(same_slot[...], low)
    inverse = jnp.where(slot_totals > 0.0, 1.0 / slot_totals, 0.0)
    weight_copy.wait()
    for h in range(HEADS):
        through = dot(segments[h], weight_buf[h * D : (h + 1) * D, :])
        projected_segs[h * SEGS : (h + 1) * SEGS, :] = (through * inverse[:, h : h + 1]).astype(BF16)
    letters = dot(jnp.concatenate([place_hot[...]] * HEADS, axis=1), projected_segs[...])
    packed[...] = jnp.where(iota((128, 128), 0) % 8 < 4, letters[:, :128], letters[:, 128:])
    for peer in row_peers:
        post(
            packed.at[pl.ds(pl.multiple_of(peer[0] * 8, 8), 8)],
            inbox.at[pl.ds(pl.multiple_of(r * 8, 8), 8)], PACK, peer,
        )
    own = pl.multiple_of(r * 8, 8)
    inbox[pl.ds(own, 8), :] = packed[pl.ds(own, 8), :]

    wait_bytes(early_in.at[pl.ds(0, ROWS - 1)], recv.at[EARLY])
    note = early_in[0]
    for k in range(1, ROWS):
        note = note + early_in[k]
    sub = iota((2 * HOME, 128), 0)
    lane = iota((2 * HOME, 128), 1)
    found = (note[:, :128] == (sub % HOME + 1).astype(F32)) & (lane // 4 % 2 == sub // HOME)
    pick = hot(found)
    home_len = jnp.sum(jnp.where(found, note[:, 128:], 0.0)[:HOME], axis=1, keepdims=True)
    seed_col = to_column(jnp.minimum(seeds[...], K).astype(F32), HOME)
    seed_hot = jnp.where(seed_col == iota((HOME, K), 1).astype(F32), 1.0, 0.0)
    home_high = jnp.floor(home_len * (1.0 / 256.0))
    group = iota((HOME, 128), 1) // HOME
    values = jnp.where(
        group == 0, home_high, jnp.where(group == 1, home_len - 256.0 * home_high, seed_col)
    )
    diagonal = iota((HOME, 128), 0) == iota((HOME, 128), 1) % HOME
    meta_own[0] = jnp.sum(jnp.where(diagonal, values, 0.0), axis=0, keepdims=True)
    metas[r] = meta_own[0]
    for peer in row_peers:
        post(meta_own.at[0], metas.at[r], META, peer)
    small_copies[4].wait()

    row_own = pl.multiple_of(c * HOME, HOME)
    col_own = pl.multiple_of(r * HOME, HOME)
    wait_bytes(inbox.at[pl.ds(0, (ROWS - 1) * 8)], recv.at[PACK])
    halves = dot(pick, inbox[...].astype(BF16))
    home_embed = jnp.concatenate([halves[:HOME], halves[HOME:]], axis=1)
    row_units[pl.ds(row_own, HOME), :] = unit_rows(home_embed).astype(BF16)
    projected = dot(home_embed.astype(BF16), plda[...])
    col_units[pl.ds(col_own, HOME), :] = unit_rows(projected).astype(BF16)
    for peer in row_peers:
        post(
            col_units.at[pl.ds(col_own, HOME)], col_units.at[pl.ds(col_own, HOME)], COLU, peer
        )
    for peer in col_peers:
        post(
            row_units.at[pl.ds(row_own, HOME)], row_units.at[pl.ds(row_own, HOME)], ROWU, peer
        )

    wait_bytes(metas.at[pl.ds(0, ROWS - 1)], recv.at[META])
    shape = (128, ROWS * HOME)
    spread_lane = iota(shape, 1) % HOME
    spread_sub = iota(shape, 0)
    take_len = jnp.where(spread_sub == spread_lane, 256.0, 0.0) + jnp.where(
        spread_sub == spread_lane + HOME, 1.0, 0.0
    )
    take_seed = jnp.where(spread_sub == spread_lane + 2 * HOME, 1.0, 0.0)
    meta_rows = jnp.concatenate([metas[k] for k in range(ROWS)], axis=0).astype(BF16)
    on_row = iota((ROWS, ROWS * HOME), 0) == iota((ROWS, ROWS * HOME), 1) // HOME

    def column_row(take):
        full = dot(meta_rows, take.astype(BF16))
        return jnp.sum(jnp.where(on_row, full, 0.0), axis=0, keepdims=True)

    len_row = column_row(take_len) * (1.0 / FPU)
    seeds_row = column_row(take_seed)
    start = jnp.where(seeds_row == iota((K, ROWS * HOME), 0).astype(F32), 1.0, 0.0).T.astype(BF16)
    for half in range(2):
        labels_buf[0, half] = start[:, half * HALF : (half + 1) * HALF]

    wait_bytes(row_units.at[pl.ds(0, (COLS - 1) * HOME)], recv.at[ROWU])
    wait_bytes(col_units.at[pl.ds(0, (ROWS - 1) * HOME)], recv.at[COLU])
    cosine = lax.dot_general(row_units[...], col_units[...], NT, preferred_element_type=F32)
    affinity[...] = (len_row * jnp.exp(cosine * (BETA / E))).astype(BF16)

    totals = None
    for step in range(ITERS):
        for half in range(2):
            if step > 0:
                wait_bytes(
                    labels_buf.at[step, half, pl.ds(0, (ROWS - 1) * HOME)],
                    recv.at[LABS + 2 * step - 2 + half],
                )
            part = dot(affinity[...], labels_buf[step, half])
            part_send[step, half] = part.astype(BF16)
            for k, peer in enumerate(col_peers):
                post(
                    part_send.at[step, half, pl.ds(pl.multiple_of(peer[1] * HOME, HOME), HOME)],
                    part_in.at[step, half, k], SUMS + 2 * step + half, peer,
                )
            parts[half] = part
        if step == 0:
            tot_send[0] = lax.dot_general(
                jnp.ones((8, ROWS * HOME), BF16), affinity[...], NT, preferred_element_type=F32
            )[0:1]
            for k, peer in enumerate(col_peers):
                post(tot_send.at[0], tot_in.at[k], TOTS, peer)
            wait_bytes(tot_in, recv.at[TOTS])
            row_totals = tot_send[0]
            for k in range(COLS - 1):
                row_totals = row_totals + tot_in[k]
            here = iota((HOME, COLS * HOME), 1) == iota((HOME, COLS * HOME), 0) + c * HOME
            totals = jnp.sum(jnp.where(here, row_totals, 0.0), axis=1, keepdims=True)
        for half in range(2):
            wait_bytes(part_in.at[step, half], recv.at[SUMS + 2 * step + half])
            spread = parts[half, pl.ds(row_own, HOME), :]
            for k in range(COLS - 1):
                spread = spread + part_in[step, half, k].astype(F32)
            labels = ALPHA * spread / totals + (1.0 - ALPHA) * seed_hot[
                :, half * HALF : (half + 1) * HALF
            ]
            if step < ITERS - 1:
                labels_buf[step + 1, half, pl.ds(col_own, HOME), :] = labels.astype(BF16)
                for peer in row_peers:
                    post(
                        labels_buf.at[step + 1, half, pl.ds(col_own, HOME)],
                        labels_buf.at[step + 1, half, pl.ds(col_own, HOME)],
                        LABS + 2 * step + half, peer,
                    )
            else:
                out[:, half * HALF : (half + 1) * HALF] = jnp.log(1.0 + K * labels)

    wait_bytes(early_in.at[pl.ds(0, ROWS - 1)], send.at[EARLY])
    wait_bytes(inbox.at[pl.ds(0, (ROWS - 1) * 8)], send.at[PACK])
    wait_bytes(row_units.at[pl.ds(0, (COLS - 1) * HOME)], send.at[ROWU])
    wait_bytes(col_units.at[pl.ds(0, (ROWS - 1) * HOME)], send.at[COLU])
    wait_bytes(metas.at[pl.ds(0, ROWS - 1)], send.at[META])
    wait_bytes(tot_in, send.at[TOTS])
    for step in range(ITERS):
        for half in range(2):
            wait_bytes(part_in.at[step, half], send.at[SUMS + 2 * step + half])
    for step in range(ITERS - 1):
        for half in range(2):
            wait_bytes(
                labels_buf.at[step + 1, half, pl.ds(0, (ROWS - 1) * HOME)],
                send.at[LABS + 2 * step + half],
            )


def on_device(frames, frame_counts, slot_ids, seed_labels, attn_query, emb_weight, plda_weight):
    vmem = pl.BlockSpec(memory_space=pltpu.VMEM)
    hbm = pl.BlockSpec(memory_space=pl.ANY)
    return pl.pallas_call(
        kernel,
        name="speaker_linking",
        out_shape=jax.ShapeDtypeStruct((HOME, K), F32),
        in_specs=[hbm] * 7,
        out_specs=vmem,
        scratch_shapes=[
            pltpu.VMEM((1, SLOTS), jnp.int32),
            pltpu.VMEM((1, SLOTS), jnp.int32),
            pltpu.VMEM((1, HOME), jnp.int32),
            pltpu.VMEM((HEADS, D), BF16),
            pltpu.VMEM((E, E), BF16),
            pltpu.VMEM((WINDOWS, WIN, D), BF16),
            pltpu.VMEM((HEADS * D, E), BF16),
            pltpu.VMEM((HEADS, SEGS, D), BF16),
            pltpu.VMEM((SEGS, 128), F32),
            pltpu.VMEM((HEADS * SEGS, E), BF16),
            pltpu.VMEM((SEGS, SEGS), BF16),
            pltpu.VMEM((SEGS, SEGS), BF16),
            pltpu.VMEM((ROWS, 1, 256), F32),
            pltpu.VMEM((ROWS, 1, 256), F32),
            pltpu.VMEM((ROWS * 8, 128), F32),
            pltpu.VMEM((ROWS * 8, 128), F32),
            pltpu.VMEM((COLS * HOME, E), BF16),
            pltpu.VMEM((ROWS * HOME, E), BF16),
            pltpu.VMEM((ROWS, 1, 128), F32),
            pltpu.VMEM((1, 1, 128), F32),
            pltpu.VMEM((COLS * HOME, ROWS * HOME), BF16),
            pltpu.VMEM((2, COLS * HOME, HALF), F32),
            pltpu.VMEM((ITERS, 2, COLS * HOME, HALF), BF16),
            pltpu.VMEM((ITERS, 2, COLS - 1, HOME, HALF), BF16),
            pltpu.VMEM((1, 1, COLS * HOME), F32),
            pltpu.VMEM((COLS - 1, 1, COLS * HOME), F32),
            pltpu.VMEM((ITERS, 2, ROWS * HOME, HALF), BF16),
            pltpu.SemaphoreType.DMA((5,)),
            pltpu.SemaphoreType.DMA((WINDOWS,)),
            pltpu.SemaphoreType.DMA,
            pltpu.SemaphoreType.DMA((N_SEMS,)),
            pltpu.SemaphoreType.DMA((N_SEMS,)),
        ],
        compiler_params=pltpu.CompilerParams(
            collective_id=0, has_side_effects=True, vmem_limit_bytes=60 * 1024 * 1024
        ),
    )(
        frames, frame_counts, slot_ids, seed_labels.reshape(1, HOME), attn_query.T, emb_weight,
        plda_weight,
    )


def solution(mesh):
    return jax.shard_map(
        on_device,
        mesh=mesh,
        in_specs=(
            P(("row", "col"), None),
            P(("row", "col"), None),
            P(("row", "col"), None),
            P(("row", "col")),
            P(),
            P(),
            P(),
        ),
        out_specs=P(("row", "col"), None),
        check_vma=False,
    )
```

```python
import jax
import jax.numpy as jnp
from jax import lax
from jax.experimental import pallas as pl
from jax.experimental.pallas import tpu as pltpu
from jax.sharding import PartitionSpec as P

MESH = pl.DeviceIdType.MESH
F32 = jnp.float32
BF16 = jnp.bfloat16

D = 1024
HEADS = 8
E = 256
K = 256
FPU = 256
SLOTS = 64
HOME = 32
ROWS = 16
COLS = 8
WIN = 1024
WINDOWS = 8
SEG = 16
SEGS = WINDOWS * SEG
ITERS = 3
HALF = 128

GAIN = 4.0
BETA = 8.0
ALPHA = 0.9
EPSILON = 1e-06

NT = (((1,), (1,)), ((), ()))

EARLY, PACK, ROWU, COLU, META, TOTS, SUMS, LABS = 0, 1, 2, 3, 4, 5, 6, 12
N_SEMS = 16


def ring(step):
    return min(step, 4 - step)


ROW_STEPS = sorted(
    [(a, b) for a in range(4) for b in range(4) if a or b], key=lambda s: -ring(s[0]) - ring(s[1])
)
COL_STEPS = sorted([(a, b) for a in range(4) for b in range(2) if a or b], key=lambda s: -ring(s[0]))


def iota(shape, dim):
    return lax.broadcasted_iota(jnp.int32, shape, dim)


def hot(condition):
    return jnp.where(condition, 1.0, 0.0).astype(BF16)


def dot(a, b):
    return jnp.dot(a, b, preferred_element_type=F32)


def to_column(row, size):
    shape = (size, row.shape[1])
    return jnp.sum(jnp.where(iota(shape, 0) == iota(shape, 1), row, 0.0), axis=1, keepdims=True)


def unit_rows(values):
    return values / jnp.sqrt(jnp.mean(values * values, axis=1, keepdims=True) + EPSILON)


def kernel(
    frames, counts_in, idents_in, seeds_in, query_in, emb_weight, plda_in, out,
    counts, idents, seeds, query, plda, frame_buf, weight_buf, segments, seg_totals, projected_segs,
    same_slot, place_hot, early_send, early_in, packed, inbox, row_units, col_units, metas, meta_own,
    affinity, parts, part_send, part_in, tot_send, tot_in, labels_buf,
    small_sem, frame_sem, weight_sem, send, recv,
):
    r = lax.axis_index("row")
    c = lax.axis_index("col")
    row_peers = [
        (lax.rem(r // 4 + a, 4) * 4 + lax.rem(lax.rem(r, 4) + b, 4), c) for a, b in ROW_STEPS
    ]
    col_peers = [
        (r, lax.rem(c // 2 + a, 4) * 2 + lax.rem(lax.rem(c, 2) + b, 2)) for a, b in COL_STEPS
    ]

    def wait_bytes(ref, sem):
        pltpu.make_async_copy(ref, ref, sem).wait()

    def post(src, dst, slot, peer):
        pltpu.make_async_remote_copy(
            src, dst, send.at[slot], recv.at[slot], device_id=peer, device_id_type=MESH
        ).start()

    def frame_copy(w):
        return pltpu.make_async_copy(
            frames.at[pl.ds(w * WIN, WIN)], frame_buf.at[w], frame_sem.at[w]
        )

    small_copies = [
        pltpu.make_async_copy(src, dst, small_sem.at[k])
        for k, (src, dst) in enumerate(
            (
                (counts_in, counts), (idents_in, idents), (query_in, query), (seeds_in, seeds),
                (plda_in, plda),
            )
        )
    ]
    for copy in small_copies[:4]:
        copy.start()
    for w in range(2):
        frame_copy(w).start()
    barrier = pltpu.get_barrier_semaphore()
    for peer in row_peers + col_peers:
        pl.semaphore_signal(barrier, inc=1, device_id=peer, device_id_type=MESH)
    for copy in small_copies[:4]:
        copy.wait()
    for w in range(2, WINDOWS):
        frame_copy(w).start()
    weight_copy = pltpu.make_async_copy(emb_weight, weight_buf, weight_sem)
    weight_copy.start()
    small_copies[4].start()

    live_row = counts[...].astype(F32)
    square = (SLOTS, SLOTS)
    ends = jnp.sum(
        jnp.where(iota(square, 1) <= iota(square, 0), live_row, 0.0), axis=1, keepdims=True
    )
    count_col = to_column(live_row, SLOTS)
    ident_row = idents[...]
    dest_row = jnp.where(counts[...] > 0, ident_row // (HOME * COLS), ROWS).astype(F32)
    dest_col = to_column(dest_row, SLOTS)
    place_col = to_column((ident_row % HOME).astype(F32), SLOTS)
    rank_col = jnp.sum(
        jnp.where((dest_col == dest_row) & (iota(square, 1) < iota(square, 0)), 1.0, 0.0),
        axis=1, keepdims=True,
    )
    wide = (SLOTS, SEGS)
    before = jnp.where(ends <= (iota(wide, 1) // SEG * WIN).astype(F32), 1.0, 0.0)
    target_row = jnp.sum(before, axis=0, keepdims=True) + (iota((1, SEGS), 1) % SEG).astype(F32)
    same_slot[...] = hot(to_column(target_row, SEGS) == target_row)
    spot = jnp.where(target_row == iota(wide, 0).astype(F32), dest_col * 8.0 + rank_col + 1.0, 0.0)
    spot_row = jnp.sum(spot, axis=0, keepdims=True) - 1.0
    letter_row = iota((SEGS, SEGS), 0)
    place_hot[...] = hot(spot_row == (letter_row // 8 * 8 + letter_row % 4).astype(F32))
    lane = iota((SLOTS, 128), 1)
    mine = (lane // 8 == r) & ((lane % 4).astype(F32) == rank_col)
    high_col = jnp.floor(count_col * (1.0 / 256.0))
    notes = jnp.concatenate(
        [jnp.where(mine, v, 0.0) for v in (place_col + 1.0, high_col, count_col - 256.0 * high_col)],
        axis=1,
    ).astype(BF16)
    notes = dot(hot(dest_row == iota((ROWS, SLOTS), 0).astype(F32)), notes)
    for k in range(ROWS):
        early_send[k] = jnp.concatenate(
            [notes[k : k + 1, :128], 256.0 * notes[k : k + 1, 128:256] + notes[k : k + 1, 256:]],
            axis=1,
        )

    query_t = query[...]

    def score(w):
        frame_copy(w).wait()
        return lax.dot_general(query_t, frame_buf[w], NT, preferred_element_type=F32)

    def pool(w, scores):
        energy = jnp.exp(GAIN * jnp.tanh(scores))
        first = (w * WIN).astype(F32)
        index = first + iota((1, WIN), 1).astype(F32)
        passed = jnp.where((ends <= index) & (ends > first), 1.0, 0.0)
        rel = jnp.sum(passed, axis=0, keepdims=True)
        mask = rel == iota((SEG, WIN), 0).astype(F32)
        rows = jnp.concatenate(
            [jnp.where(mask, energy[h : h + 1, :], 0.0) for h in range(HEADS)], axis=0
        )
        sums = jnp.sum(rows, axis=1, keepdims=True)
        totals = jnp.zeros((SEG, 128), F32)
        for h in range(HEADS):
            totals = jnp.where(iota((SEG, 128), 1) == h, sums[h * SEG : (h + 1) * SEG], totals)
        seg_totals[pl.ds(pl.multiple_of(w * SEG, SEG), SEG), :] = totals
        pooled = dot(rows.astype(BF16), frame_buf[w])
        for h in range(HEADS):
            segments[h, pl.ds(pl.multiple_of(w * SEG, SEG), SEG), :] = pooled[
                h * SEG : (h + 1) * SEG
            ].astype(BF16)

    def two_windows(t, carry):
        first = score(2 * t)
        second = score(2 * t + 1)
        pool(2 * t, first)
        pool(2 * t + 1, second)
        return carry

    lax.fori_loop(0, WINDOWS // 4, two_windows, 0)
    pl.semaphore_wait(barrier, ROWS + COLS - 2)
    for peer in row_peers:
        post(early_send.at[peer[0]], early_in.at[r], EARLY, peer)
    early_in[r] = early_send[r]
    lax.fori_loop(WINDOWS // 4, WINDOWS // 2, two_windows, 0)

    high = seg_totals[...].astype(BF16)
    low = (seg_totals[...] - high.astype(F32)).astype(BF16)
    slot_totals = dot(same_slot[...], high) + dot(same_slot[...], low)
    inverse = jnp.where(slot_totals > 0.0, 1.0 / slot_totals, 0.0)
    weight_copy.wait()
    for h in range(HEADS):
        through = dot(segments[h], weight_buf[h * D : (h + 1) * D, :])
        projected_segs[h * SEGS : (h + 1) * SEGS, :] = (through * inverse[:, h : h + 1]).astype(BF16)
    letters = dot(jnp.concatenate([place_hot[...]] * HEADS, axis=1), projected_segs[...])
    packed[...] = jnp.where(iota((128, 128), 0) % 8 < 4, letters[:, :128], letters[:, 128:])
    for peer in row_peers:
        post(
            packed.at[pl.ds(pl.multiple_of(peer[0] * 8, 8), 8)],
            inbox.at[pl.ds(pl.multiple_of(r * 8, 8), 8)], PACK, peer,
        )
    own = pl.multiple_of(r * 8, 8)
    inbox[pl.ds(own, 8), :] = packed[pl.ds(own, 8), :]

    wait_bytes(early_in.at[pl.ds(0, ROWS - 1)], recv.at[EARLY])
    note = early_in[0]
    for k in range(1, ROWS):
        note = note + early_in[k]
    sub = iota((2 * HOME, 128), 0)
    lane = iota((2 * HOME, 128), 1)
    found = (note[:, :128] == (sub % HOME + 1).astype(F32)) & (lane // 4 % 2 == sub // HOME)
    pick = hot(found)
    home_len = jnp.sum(jnp.where(found, note[:, 128:], 0.0)[:HOME], axis=1, keepdims=True)
    seed_col = to_column(jnp.minimum(seeds[...], K).astype(F32), HOME)
    seed_hot = jnp.where(seed_col == iota((HOME, K), 1).astype(F32), 1.0, 0.0)
    home_high = jnp.floor(home_len * (1.0 / 256.0))
    group = iota((HOME, 128), 1) // HOME
    values = jnp.where(
        group == 0, home_high, jnp.where(group == 1, home_len - 256.0 * home_high, seed_col)
    )
    diagonal = iota((HOME, 128), 0) == iota((HOME, 128), 1) % HOME
    meta_own[0] = jnp.sum(jnp.where(diagonal, values, 0.0), axis=0, keepdims=True)
    metas[r] = meta_own[0]
    for peer in row_peers:
        post(meta_own.at[0], metas.at[r], META, peer)
    small_copies[4].wait()

    row_own = pl.multiple_of(c * HOME, HOME)
    col_own = pl.multiple_of(r * HOME, HOME)
    wait_bytes(inbox.at[pl.ds(0, (ROWS - 1) * 8)], recv.at[PACK])
    halves = dot(pick, inbox[...].astype(BF16))
    home_embed = jnp.concatenate([halves[:HOME], halves[HOME:]], axis=1)
    row_units[pl.ds(row_own, HOME), :] = unit_rows(home_embed).astype(BF16)
    projected = dot(home_embed.astype(BF16), plda[...])
    col_units[pl.ds(col_own, HOME), :] = unit_rows(projected).astype(BF16)
    for peer in row_peers:
        post(
            col_units.at[pl.ds(col_own, HOME)], col_units.at[pl.ds(col_own, HOME)], COLU, peer
        )
    for peer in col_peers:
        post(
            row_units.at[pl.ds(row_own, HOME)], row_units.at[pl.ds(row_own, HOME)], ROWU, peer
        )

    wait_bytes(metas.at[pl.ds(0, ROWS - 1)], recv.at[META])
    shape = (128, ROWS * HOME)
    spread_lane = iota(shape, 1) % HOME
    spread_sub = iota(shape, 0)
    take_len = jnp.where(spread_sub == spread_lane, 256.0, 0.0) + jnp.where(
        spread_sub == spread_lane + HOME, 1.0, 0.0
    )
    take_seed = jnp.where(spread_sub == spread_lane + 2 * HOME, 1.0, 0.0)
    meta_rows = jnp.concatenate([metas[k] for k in range(ROWS)], axis=0).astype(BF16)
    on_row = iota((ROWS, ROWS * HOME), 0) == iota((ROWS, ROWS * HOME), 1) // HOME

    def column_row(take):
        full = dot(meta_rows, take.astype(BF16))
        return jnp.sum(jnp.where(on_row, full, 0.0), axis=0, keepdims=True)

    len_row = column_row(take_len) * (1.0 / FPU)
    seeds_row = column_row(take_seed)
    start = jnp.where(seeds_row == iota((K, ROWS * HOME), 0).astype(F32), 1.0, 0.0).T.astype(BF16)
    for half in range(2):
        labels_buf[0, half] = start[:, half * HALF : (half + 1) * HALF]

    wait_bytes(row_units.at[pl.ds(0, (COLS - 1) * HOME)], recv.at[ROWU])
    wait_bytes(col_units.at[pl.ds(0, (ROWS - 1) * HOME)], recv.at[COLU])
    cosine = lax.dot_general(row_units[...], col_units[...], NT, preferred_element_type=F32)
    affinity[...] = (len_row * jnp.exp(cosine * (BETA / E))).astype(BF16)

    totals = None
    for step in range(ITERS):
        for half in range(2):
            if step > 0:
                wait_bytes(
                    labels_buf.at[step, half, pl.ds(0, (ROWS - 1) * HOME)],
                    recv.at[LABS + 2 * step - 2 + half],
                )
            part = dot(affinity[...], labels_buf[step, half])
            part_send[step, half] = part.astype(BF16)
            for k, peer in enumerate(col_peers):
                post(
                    part_send.at[step, half, pl.ds(pl.multiple_of(peer[1] * HOME, HOME), HOME)],
                    part_in.at[step, half, k], SUMS + 2 * step + half, peer,
                )
            parts[half] = part
        if step == 0:
            tot_send[0] = lax.dot_general(
                jnp.ones((8, ROWS * HOME), BF16), affinity[...], NT, preferred_element_type=F32
            )[0:1]
            for k, peer in enumerate(col_peers):
                post(tot_send.at[0], tot_in.at[k], TOTS, peer)
            wait_bytes(tot_in, recv.at[TOTS])
            row_totals = tot_send[0]
            for k in range(COLS - 1):
                row_totals = row_totals + tot_in[k]
            here = iota((HOME, COLS * HOME), 1) == iota((HOME, COLS * HOME), 0) + c * HOME
            totals = jnp.sum(jnp.where(here, row_totals, 0.0), axis=1, keepdims=True)
        for half in range(2):
            wait_bytes(part_in.at[step, half], recv.at[SUMS + 2 * step + half])
            spread = parts[half, pl.ds(row_own, HOME), :]
            for k in range(COLS - 1):
                spread = spread + part_in[step, half, k].astype(F32)
            labels = ALPHA * spread / totals + (1.0 - ALPHA) * seed_hot[
                :, half * HALF : (half + 1) * HALF
            ]
            if step < ITERS - 1:
                labels_buf[step + 1, half, pl.ds(col_own, HOME), :] = labels.astype(BF16)
                for peer in row_peers:
                    post(
                        labels_buf.at[step + 1, half, pl.ds(col_own, HOME)],
                        labels_buf.at[step + 1, half, pl.ds(col_own, HOME)],
                        LABS + 2 * step + half, peer,
                    )
            else:
                out[:, half * HALF : (half + 1) * HALF] = jnp.log(1.0 + K * labels)

    wait_bytes(early_in.at[pl.ds(0, ROWS - 1)], send.at[EARLY])
    wait_bytes(inbox.at[pl.ds(0, (ROWS - 1) * 8)], send.at[PACK])
    wait_bytes(row_units.at[pl.ds(0, (COLS - 1) * HOME)], send.at[ROWU])
    wait_bytes(col_units.at[pl.ds(0, (ROWS - 1) * HOME)], send.at[COLU])
    wait_bytes(metas.at[pl.ds(0, ROWS - 1)], send.at[META])
    wait_bytes(tot_in, send.at[TOTS])
    for step in range(ITERS):
        for half in range(2):
            wait_bytes(part_in.at[step, half], send.at[SUMS + 2 * step + half])
    for step in range(ITERS - 1):
        for half in range(2):
            wait_bytes(
                labels_buf.at[step + 1, half, pl.ds(0, (ROWS - 1) * HOME)],
                send.at[LABS + 2 * step + half],
            )


def on_device(frames, frame_counts, slot_ids, seed_labels, attn_query, emb_weight, plda_weight):
    vmem = pl.BlockSpec(memory_space=pltpu.VMEM)
    hbm = pl.BlockSpec(memory_space=pl.ANY)
    return pl.pallas_call(
        kernel,
        name="speaker_linking",
        out_shape=pltpu.VMEM((HOME, K), F32),
        in_specs=[hbm] * 7,
        out_specs=vmem,
        scratch_shapes=[
            pltpu.VMEM((1, SLOTS), jnp.int32),
            pltpu.VMEM((1, SLOTS), jnp.int32),
            pltpu.VMEM((1, HOME), jnp.int32),
            pltpu.VMEM((HEADS, D), BF16),
            pltpu.VMEM((E, E), BF16),
            pltpu.VMEM((WINDOWS, WIN, D), BF16),
            pltpu.VMEM((HEADS * D, E), BF16),
            pltpu.VMEM((HEADS, SEGS, D), BF16),
            pltpu.VMEM((SEGS, 128), F32),
            pltpu.VMEM((HEADS * SEGS, E), BF16),
            pltpu.VMEM((SEGS, SEGS), BF16),
            pltpu.VMEM((SEGS, SEGS), BF16),
            pltpu.VMEM((ROWS, 1, 256), F32),
            pltpu.VMEM((ROWS, 1, 256), F32),
            pltpu.VMEM((ROWS * 8, 128), F32),
            pltpu.VMEM((ROWS * 8, 128), F32),
            pltpu.VMEM((COLS * HOME, E), BF16),
            pltpu.VMEM((ROWS * HOME, E), BF16),
            pltpu.VMEM((ROWS, 1, 128), F32),
            pltpu.VMEM((1, 1, 128), F32),
            pltpu.VMEM((COLS * HOME, ROWS * HOME), BF16),
            pltpu.VMEM((2, COLS * HOME, HALF), F32),
            pltpu.VMEM((ITERS, 2, COLS * HOME, HALF), BF16),
            pltpu.VMEM((ITERS, 2, COLS - 1, HOME, HALF), BF16),
            pltpu.VMEM((1, 1, COLS * HOME), F32),
            pltpu.VMEM((COLS - 1, 1, COLS * HOME), F32),
            pltpu.VMEM((ITERS, 2, ROWS * HOME, HALF), BF16),
            pltpu.SemaphoreType.DMA((5,)),
            pltpu.SemaphoreType.DMA((WINDOWS,)),
            pltpu.SemaphoreType.DMA,
            pltpu.SemaphoreType.DMA((N_SEMS,)),
            pltpu.SemaphoreType.DMA((N_SEMS,)),
        ],
        compiler_params=pltpu.CompilerParams(
            collective_id=0, has_side_effects=True, vmem_limit_bytes=60 * 1024 * 1024
        ),
    )(
        frames, frame_counts, slot_ids, seed_labels.reshape(1, HOME), attn_query.T, emb_weight,
        plda_weight,
    )


def solution(mesh):
    return jax.shard_map(
        on_device,
        mesh=mesh,
        in_specs=(
            P(("row", "col"), None),
            P(("row", "col"), None),
            P(("row", "col"), None),
            P(("row", "col")),
            P(),
            P(),
            P(),
        ),
        out_specs=P(("row", "col"), None),
        check_vma=False,
    )
```
